32 devices in a mesh: region: 4 (over x, core), dev: 8 (over z, y).
Axes of the slice: x: 2, y: 2, z: 4, core: 2. Of those that a mesh axis runs over, the one named last changes fastest.
Arguments:
- synthetic: bfloat16 [512, 3, 4096], P(('region', 'dev')), may hold values from -6 to 6
- observed: bfloat16 [512, 3, 4096], P(('region', 'dev')), may hold values from -6 to 6
- nearby_receiver_slots: int32 [256, 4], P(('region', 'dev')), may hold values from 0 to 15
- far_rows: int32 [256, 4], P(('region', 'dev')), may hold values from 0 to 15
- first_slot: int32 [8192], P(('region', 'dev')), may hold values from 0 to 31
- second_slot: int32 [8192], P(('region', 'dev')), may hold values from 0 to 63
- window_start: int32 [8192], P(('region', 'dev')), may hold values from 0 to 255
- pair_delay_indices: int32 [8192], P(('region', 'dev')), may hold values from 64 to 256
Outputs:
- adjoint: bfloat16 [512, 3, 4096], P(('region', 'dev'))
- misfit: float32 [8192], P(('region', 'dev'))
The draws below stay inside these ranges and needn't reach their ends.
All inputs are finite; a program needn't handle non-finite values.
Results may differ from the reference program's by a relative error of at most 0.0084.
Values may be sent and summed in bfloat16 or wider, within the bound.
A program may use at most 128 MiB of HBM per device.

```python
import math
import jax
import jax.numpy as jnp
from jax import lax

NT = 4096
F = 512
FLOW = 64
LAGS = 512
RPD = 16
CAP = 4
PAIRS_DEV = 256
STATION_TOTAL = 512
PAIRS = 8192
N_REGION = 4
N_DEV = 8
DEVICES = 32


def place_ends(entries, stream_key, least, top_value):
    longest = entries.shape.index(max(entries.shape))
    spots = []
    for shift in (0, 1):
        where = [jax.random.randint(jax.random.fold_in(stream_key, axis), (), 0, length) for axis, length in enumerate(entries.shape)]
        where[longest] = (where[longest] + shift) % entries.shape[longest]
        spots.append(tuple(where))
    return entries.at[spots[0]].set(least).at[spots[1]].set(top_value)


def level_of(key, extent, shards, smallest, top_value):
    loudness, own = 1.0, jax.random.fold_in(key, 6)
    for axis_at, parts in shards:
        steps = jnp.exp(jax.random.uniform(jax.random.fold_in(own, axis_at), (parts,), jnp.float32, smallest / len(shards), top_value / len(shards)))
        loudness = loudness * jnp.repeat(steps, extent[axis_at] // parts).reshape([-1 if axis == axis_at else 1 for axis in range(len(extent))])
    return loudness


def gaussian(own_key, extent, spread, most, split=(), kind=jnp.bfloat16):
    loudness = level_of(own_key, extent, split, -0.22, 0.18) if split else 1.0
    entries = jax.random.normal(own_key, extent, jnp.float32) * spread * loudness
    return jnp.minimum(jnp.maximum(entries, -most), most).astype(kind)


def setup_inputs(seed: int = 0) -> dict:
    seeds = jax.random.split(jax.random.key(seed), 9)
    synthetic = gaussian(seeds[0], (STATION_TOTAL, 3, NT), 1.0, 6.0, ((0, 32),))
    observed = gaussian(seeds[1], (STATION_TOTAL, 3, NT), 1.0, 6.0, ((0, 32),))
    nearby_receiver_slots = place_ends(jax.random.randint(seeds[2], (DEVICES * N_DEV, CAP), 0, RPD), jax.random.fold_in(seeds[2], 1), 0, RPD - 1).astype(jnp.int32)
    far_rows = place_ends(jax.random.randint(seeds[3], (DEVICES * N_DEV, CAP), 0, RPD), jax.random.fold_in(seeds[3], 1), 0, RPD - 1).astype(jnp.int32)
    first_slot = place_ends(jax.random.randint(seeds[4], (PAIRS,), 0, N_DEV * CAP), jax.random.fold_in(seeds[4], 1), 0, (N_DEV * CAP) - 1).astype(jnp.int32)
    second_slot = place_ends(jax.random.randint(seeds[5], (PAIRS,), 0, 2 * N_DEV * CAP), jax.random.fold_in(seeds[5], 1), 0, (2 * N_DEV * CAP) - 1).astype(jnp.int32)
    window_start = place_ends(jax.random.randint(seeds[6], (PAIRS,), 0, LAGS // 2), jax.random.fold_in(seeds[6], 1), 0, (LAGS // 2) - 1).astype(jnp.int32)
    pair_delay_indices = place_ends(jax.random.randint(seeds[7], (PAIRS,), LAGS // 8, LAGS // 2 + 1), jax.random.fold_in(seeds[7], 1), LAGS // 8, (LAGS // 2 + 1) - 1).astype(jnp.int32)
    return dict(synthetic=synthetic, observed=observed, nearby_receiver_slots=nearby_receiver_slots, far_rows=far_rows, first_slot=first_slot, second_slot=second_slot, window_start=window_start, pair_delay_indices=pair_delay_indices)


def make_tables(discrete_ticks):
    clock_moments = jnp.arange(discrete_ticks, dtype=jnp.int32)
    angular_rate = FLOW + jnp.arange(F, dtype=jnp.int32)
    oscillation_arguments = clock_moments[:, None] * angular_rate[None, :] % discrete_ticks
    angles = oscillation_arguments.astype(jnp.float32) * (2.0 * math.pi / discrete_ticks)
    forward = (jnp.concatenate([jnp.cos(angles), -jnp.sin(angles)], 1) / math.sqrt(discrete_ticks)).astype(jnp.bfloat16)
    shifts = jnp.arange(LAGS, dtype=jnp.int32) - LAGS // 2
    turning = angular_rate[:, None] * shifts[None, :] % discrete_ticks
    delay_rotation_matrix = turning.astype(jnp.float32) * (2.0 * math.pi / discrete_ticks)
    lag_lookup_table = (jnp.concatenate([jnp.cos(delay_rotation_matrix), -jnp.sin(delay_rotation_matrix)], 0) / math.sqrt(F)).astype(jnp.bfloat16)
    return (forward, lag_lookup_table)

def cross_power_spectrum(left, right):
    left_re, left_im = (left[..., :F], left[..., F:])
    right_re, right_im = (right[..., :F], right[..., F:])
    return jnp.concatenate([left_re * right_re + left_im * right_im, left_im * right_re - left_re * right_im], -1)

def pair_terms(first, second, starts, lengths, lag_lookup_table):
    first = first.astype(jnp.float32)
    second = second.astype(jnp.float32)
    change = (cross_power_spectrum(first[:, 0], second[:, 0]) - cross_power_spectrum(first[:, 1], second[:, 1])).astype(jnp.bfloat16)
    count = change.shape[0]
    shifted = jnp.dot(change.reshape(count * 3, 2 * F), lag_lookup_table, preferred_element_type=jnp.float32).reshape(count, 3, LAGS)
    position = jnp.arange(LAGS, dtype=jnp.int32)
    inside = (position[None, :] >= starts[:, None]) & (position[None, :] < (starts + lengths)[:, None])
    residual = jnp.where(inside[:, None, :], shifted, 0.0)
    misfit = lax.optimization_barrier(jnp.sum(residual * residual, axis=(1, 2))) / (2.0 * LAGS)
    slope = lax.dot_general(residual.astype(jnp.bfloat16).reshape(count * 3, LAGS), lag_lookup_table, (((1,), (1,)), ((), ())), preferred_element_type=jnp.float32).reshape(count, 3, 2 * F)
    slope_re, slope_im = (slope[..., :F], slope[..., F:])
    first_re, first_im = (first[:, 0, :, :F], first[:, 0, :, F:])
    second_re, second_im = (second[:, 0, :, :F], second[:, 0, :, F:])
    grad_first = jnp.concatenate([slope_re * second_re - slope_im * second_im, slope_re * second_im + slope_im * second_re], -1)
    grad_second = jnp.concatenate([slope_re * first_re + slope_im * first_im, slope_re * first_im - slope_im * first_re], -1)
    return (misfit, grad_first, grad_second)

def reference(synthetic, observed, nearby_receiver_slots, far_rows, first_slot, second_slot, window_start, pair_delay_indices):
    discrete_ticks = synthetic.shape[2]
    forward, lag_lookup_table = make_tables(discrete_ticks)

    def transform(traces):
        stacked = jnp.stack([traces[0], traces[1]], 1).reshape(RPD * 6, discrete_ticks)
        return jnp.dot(stacked, forward, preferred_element_type=jnp.float32).astype(jnp.bfloat16).reshape(RPD, 2, 3, 2 * F)
    spectra = lax.map(transform, (synthetic.reshape(DEVICES, RPD, 3, discrete_ticks), observed.reshape(DEVICES, RPD, 3, discrete_ticks)))
    spectra = spectra.reshape(N_REGION, N_DEV, RPD, 2, 3, 2 * F)
    padded = jnp.concatenate([spectra, jnp.zeros_like(spectra[:1])], 0)
    near_table = nearby_receiver_slots.reshape(N_REGION, N_DEV, N_DEV, CAP)
    far_table = far_rows.reshape(N_REGION, N_DEV, N_DEV, CAP)
    slot_count = 2 * N_DEV * CAP
    peer_index = jnp.arange(N_DEV, dtype=jnp.int32)[:, None]

    def visit(totals, owner):
        region = owner // N_DEV
        member = owner % N_DEV
        here = lax.dynamic_index_in_dim(padded, region, 0, keepdims=False)
        there = lax.dynamic_index_in_dim(padded, region + 1, 0, keepdims=False)
        near_pick = lax.dynamic_index_in_dim(near_table, region, 0, keepdims=False)[:, member, :]
        far_pick = lax.dynamic_index_in_dim(far_table, region, 0, keepdims=False)[:, member, :]
        fetched = jnp.concatenate([here[peer_index, near_pick], there[peer_index, far_pick]], 0).reshape(slot_count, 2, 3, 2 * F)
        begin = owner * PAIRS_DEV
        first_ids = lax.dynamic_slice_in_dim(first_slot, begin, PAIRS_DEV)
        second_ids = lax.dynamic_slice_in_dim(second_slot, begin, PAIRS_DEV)
        starts = lax.dynamic_slice_in_dim(window_start, begin, PAIRS_DEV)
        lengths = lax.dynamic_slice_in_dim(pair_delay_indices, begin, PAIRS_DEV)
        misfit, grad_first, grad_second = pair_terms(fetched[first_ids], fetched[second_ids], starts, lengths, lag_lookup_table)
        slot_grad = jax.ops.segment_sum(jnp.concatenate([grad_first, grad_second], 0), jnp.concatenate([first_ids, second_ids], 0), num_segments=slot_count).reshape(2, N_DEV, CAP, 3, 2 * F)
        totals = totals.at[region, peer_index, near_pick].add(slot_grad[0])
        totals = totals.at[region + 1, peer_index, far_pick].add(slot_grad[1])
        return (totals, misfit)
    start_totals = jnp.zeros((N_REGION + 1, N_DEV, RPD, 3, 2 * F), jnp.float32)
    totals, misfits = lax.scan(visit, start_totals, jnp.arange(DEVICES, dtype=jnp.int32))
    gathered = totals[:N_REGION].reshape(DEVICES, RPD * 3, 2 * F).astype(jnp.bfloat16)

    def reciprocal_factor(block):
        return lax.dot_general(block, forward, (((1,), (1,)), ((), ())), preferred_element_type=jnp.float32).astype(jnp.bfloat16)
    adjoint = lax.map(reciprocal_factor, gathered).reshape(STATION_TOTAL, 3, discrete_ticks)
    return (adjoint, misfits.reshape(PAIRS))
```

```python
import functools
import math

import jax
import jax.numpy as jnp
import ml_dtypes
import numpy as np
from jax import lax
from jax.experimental import pallas as pl
from jax.experimental.pallas import tpu as pltpu
from jax.sharding import PartitionSpec as P

F = 512
FLOW = 64
LAGS = 512
BLOCK = 256
MESH = pl.DeviceIdType.MESH


def make_tables(ticks):
    rate = FLOW + np.arange(F, dtype=np.int64)
    angles = (np.arange(ticks)[:, None] * rate[None, :] % ticks) * (2.0 * math.pi / ticks)
    forward = np.concatenate([np.cos(angles), -np.sin(angles)], 1) / math.sqrt(ticks)
    shifts = np.arange(LAGS, dtype=np.int64) - LAGS // 2
    turning = (rate[:, None] * shifts[None, :] % ticks) * (2.0 * math.pi / ticks)
    lag = np.concatenate([np.cos(turning), -np.sin(turning)], 0) / math.sqrt(F)
    short = lambda x: x.astype(np.float32).astype(ml_dtypes.bfloat16)
    return short(forward), short(lag)


def dot(a, b):
    return jnp.dot(a, b, preferred_element_type=jnp.float32)


def one_hot(condition):
    return jnp.where(condition, 1.0, 0.0).astype(jnp.bfloat16)


def iota(shape, axis):
    return lax.broadcasted_iota(jnp.int32, shape, axis)


def down(row, width):
    pairs = row.shape[1]
    column = jnp.transpose(jnp.broadcast_to(row.astype(jnp.float32), (128, pairs)))
    return jnp.concatenate([column] * (width // 128), 1).astype(jnp.int32)


def kernel(
    regions, peers, cap, local,
    syn_ref, obs_ref, near_ref, far_ref, first_ref, second_ref, start_ref, length_ref,
    w_hbm, wt_hbm, lag_hbm, lagt_hbm,
    adj_ref, misfit_ref,
    w, wt, lag, lagt, far_in, sp, send, recv, gout, gin, own, pick, spread, sel_out, sel_in,
    inside, energy, grads,
    w_sem, table_sem, idx_send, idx_recv, send_sem, recv_sem, gsend_sem, grecv_sem,
):
    region, me = lax.axis_index("region"), lax.axis_index("dev")
    last = regions - 1
    sources = 2 * peers
    rows = sources * 16
    pairs = first_ref.shape[1]

    w_copies = [pltpu.make_async_copy(w_hbm.at[i], w.at[i], w_sem.at[i]) for i in range(4)]
    table_copies = [
        pltpu.make_async_copy(a, b, table_sem.at[i])
        for i, (a, b) in enumerate(((lag_hbm, lag), (lagt_hbm, lagt), (wt_hbm, wt)))
    ]
    for copy in w_copies + table_copies:
        copy.start()

    barrier = pltpu.get_barrier_semaphore()

    def greet(j, carry):
        @pl.when(j != me)
        def _():
            pl.semaphore_signal(barrier, inc=1, device_id=(region, j), device_id_type=MESH)

        @pl.when(region > 0)
        def _():
            pl.semaphore_signal(barrier, inc=1, device_id=(region - 1, j), device_id_type=MESH)

        @pl.when(region < last)
        def _():
            pl.semaphore_signal(barrier, inc=1, device_id=(region + 1, j), device_id_type=MESH)

        return carry

    lax.fori_loop(0, peers, greet, 0)
    below = jnp.where(region > 0, peers, 0)
    above = jnp.where(region < last, peers, 0)
    pl.semaphore_wait(barrier, peers - 1 + below + above)

    def idx_copy(target):
        return pltpu.make_async_remote_copy(
            src_ref=far_ref, dst_ref=far_in, send_sem=idx_send, recv_sem=idx_recv,
            device_id=(target, me), device_id_type=MESH,
        )

    @pl.when(region < last)
    def _():
        idx_copy(region + 1).start()

    @pl.when(region == 0)
    def _():
        far_in[...] = jnp.zeros_like(far_in)
        gin[:, peers:sources] = jnp.zeros((3, peers, 16, BLOCK), jnp.bfloat16)

    @pl.when(region == last)
    def _():
        recv[:, peers:sources] = jnp.zeros((3, peers, 16, F), jnp.bfloat16)

    for end, ref in enumerate((first_ref, second_ref)):
        slot = ref[...]
        base = (slot >> 2) * 16 + (slot & 3)
        column = down(base, rows)
        lanes = iota((pairs, rows), 1)
        ups = iota((rows, pairs), 0)
        for o in range(4):
            at = (end * 4 + o) * pairs
            pick[at : at + pairs, :] = one_hot(lanes == column + 4 * o)
            spread[:, at : at + pairs] = one_hot(ups == base + 4 * o)
    position = iota((pairs, LAGS), 1)
    begin = down(start_ref[...], LAGS)
    stop = down(start_ref[...] + length_ref[...], LAGS)
    inside[...] = jnp.where((position >= begin) & (position < stop), 1.0, 0.0)
    energy[...] = jnp.zeros_like(energy)

    x = jnp.concatenate(
        [syn_ref[...].reshape(3 * local, -1), obs_ref[...].reshape(3 * local, -1)], 0
    )
    for i in range(4):
        w_copies[i].wait()
        part, half = i // 2, i % 2
        y = dot(x, w[i]).astype(jnp.bfloat16)
        for k in range(2):
            for c in range(3):
                at = part * 32 + k * 16
                sp[c, at : at + 16, half * BLOCK : (half + 1) * BLOCK] = y[
                    k * 48 + c * 16 : k * 48 + c * 16 + 16
                ]

    @pl.when(region > 0)
    def _():
        idx_copy(region).wait_recv()

    near_owner = jnp.where(iota((peers, rows), 1) // 16 == iota((peers, rows), 0), 1.0, 0.0)
    far_owner = jnp.where(
        iota((peers, rows), 1) // 16 == iota((peers, rows), 0) + peers, 1.0, 0.0
    )
    wide = dot(near_ref[...].astype(jnp.float32), near_owner)
    wide += dot(far_in[...].astype(jnp.float32), far_owner)
    wide = jnp.where(iota((cap, rows), 1) % 4 == iota((cap, rows), 0), wide, 0.0)
    asked_row = jnp.broadcast_to(jnp.sum(wide, 0, keepdims=True), (128, rows))
    asked_col = jnp.transpose(asked_row)
    asked_row = asked_row[:64].astype(jnp.int32)
    row = iota((rows, 64), 0)
    column = (row // 4 % 2) * 32 + (row // 8 % 2) * 16 + asked_col[:, :64].astype(jnp.int32)
    sel_out[...] = one_hot(column == iota((rows, 64), 1))
    up = iota((64, rows), 0)
    sel_in[...] = one_hot((asked_row == up % 16) & (iota((64, rows), 1) // 4 % 4 == up // 16))

    def spectra_copy(c, to, src, dst, target):
        return pltpu.make_async_remote_copy(
            src_ref=send.at[c, src], dst_ref=recv.at[c, dst],
            send_sem=send_sem.at[c, src], recv_sem=recv_sem.at[c, dst],
            device_id=(to, target), device_id_type=MESH,
        )

    def grad_copy(c, to, src, dst, target):
        return pltpu.make_async_remote_copy(
            src_ref=gout.at[c, src], dst_ref=gin.at[c, dst],
            send_sem=gsend_sem.at[c, src], recv_sem=grecv_sem.at[c, dst],
            device_id=(to, target), device_id_type=MESH,
        )

    def exchange(c, carry):
        block = dot(sel_out[...], sp[c]).astype(jnp.bfloat16)
        send[c] = block.reshape(sources, 16, F)
        recv[c, me] = send[c, me]

        def go(i, carry):
            j = (me + 1 + i) % peers

            @pl.when(j != me)
            def _():
                spectra_copy(c, region, j, me, j).start()

            @pl.when(region > 0)
            def _():
                spectra_copy(c, region - 1, peers + j, peers + me, j).start()

            return carry

        return lax.fori_loop(0, peers, go, carry)

    lax.fori_loop(0, 3, exchange, 0)

    table_copies[0].wait()
    table_copies[1].wait()

    def work(c, carry):
        def arrive(j, carry):
            @pl.when(j != me)
            def _():
                spectra_copy(c, region, j, j, j).wait_recv()

            @pl.when(region < last)
            def _():
                spectra_copy(c, region, peers + j, peers + j, j).wait_recv()

            return carry

        lax.fori_loop(0, peers, arrive, 0)
        fetched = recv[c].reshape(rows, F)
        got = lambda end, o: dot(pick[(end * 4 + o) * pairs : (end * 4 + o + 1) * pairs], fetched)
        ar, ai, br, bi = got(0, 0), got(0, 1), got(1, 0), got(1, 1)
        ur, ui, vr, vi = got(0, 2), got(0, 3), got(1, 2), got(1, 3)
        change_re = ((ar * br + ai * bi) - (ur * vr + ui * vi)).astype(jnp.bfloat16)
        change_im = ((ai * br - ar * bi) - (ui * vr - ur * vi)).astype(jnp.bfloat16)
        shifted = dot(change_re, lag[:F]) + dot(change_im, lag[F:])
        residual = jnp.where(inside[...] > 0.5, shifted, 0.0)
        energy[...] += residual * residual
        short = residual.astype(jnp.bfloat16)
        gr, gi = dot(short, lagt[:, :F]), dot(short, lagt[:, F:])
        ends = (
            (gr * br - gi * bi, gr * bi + gi * br),
            (gr * ar + gi * ai, gr * ai - gi * ar),
        )
        for end in range(2):
            for part in range(2):
                value = ends[end][part].astype(jnp.bfloat16)
                for half in range(2):
                    at = (end * 4 + half * 2 + part) * pairs
                    grads[at : at + pairs] = value[:, half * BLOCK : (half + 1) * BLOCK]
        total = dot(spread[...], grads[...]).astype(jnp.bfloat16)
        gout[c] = total.reshape(sources, 16, BLOCK)
        gin[c, me] = gout[c, me]

        def go(i, carry):
            j = (me + 1 + i) % peers

            @pl.when(j != me)
            def _():
                grad_copy(c, region, j, me, j).start()

            @pl.when(region < last)
            def _():
                grad_copy(c, region + 1, peers + j, peers + me, j).start()

            return carry

        return lax.fori_loop(0, peers, go, carry)

    lax.fori_loop(0, 3, work, 0)

    power = energy[:, :128]
    for i in range(1, LAGS // 128):
        power = power + energy[:, i * 128 : (i + 1) * 128]
    misfit_ref[...] = jnp.sum(jnp.transpose(power), 0, keepdims=True) / (2.0 * LAGS)

    def settle(c, carry):
        def arrive(j, carry):
            @pl.when(j != me)
            def _():
                grad_copy(c, region, j, j, j).wait_recv()

            @pl.when(region > 0)
            def _():
                grad_copy(c, region, peers + j, peers + j, j).wait_recv()

            return carry

        lax.fori_loop(0, peers, arrive, 0)
        total = dot(sel_in[...], gin[c].reshape(rows, BLOCK)).astype(jnp.bfloat16)
        for half in range(2):
            for part in range(2):
                o = half * 2 + part
                at = part * F + half * BLOCK
                own[c, :, at : at + BLOCK] = total[o * 16 : o * 16 + 16]
        return carry

    lax.fori_loop(0, 3, settle, 0)

    table_copies[2].wait()
    gathered = own[...].reshape(3 * local, 2 * F)
    width = wt.shape[2]

    def back(i, carry):
        at = pl.ds(pl.multiple_of(i * width, width), width)
        adj_ref[:, at] = dot(gathered, wt[i]).astype(jnp.bfloat16)
        return carry

    lax.fori_loop(0, wt.shape[0], back, 0)

    def sent(i, carry):
        c, j = i // peers, i % peers

        @pl.when(j != me)
        def _():
            spectra_copy(c, region, j, j, j).wait_send()
            grad_copy(c, region, j, j, j).wait_send()

        @pl.when(region > 0)
        def _():
            spectra_copy(c, region, peers + j, peers + j, j).wait_send()

        @pl.when(region < last)
        def _():
            grad_copy(c, region, peers + j, peers + j, j).wait_send()

        return carry

    lax.fori_loop(0, 3 * peers, sent, 0)

    @pl.when(region < last)
    def _():
        idx_copy(region).wait_send()


def on_device(
    regions, peers, synthetic, observed, nearby, far_rows, first, second, start, length
):
    local, _, ticks = synthetic.shape
    cap = nearby.shape[1]
    pairs = first.shape[0]
    forward, lag = make_tables(ticks)
    w = jnp.asarray(np.ascontiguousarray(forward.reshape(ticks, 4, BLOCK).transpose(1, 0, 2)))
    wt = jnp.asarray(
        np.ascontiguousarray(forward.T.reshape(2 * F, ticks // 512, 512).transpose(1, 0, 2))
    )
    lagt = jnp.asarray(np.ascontiguousarray(lag.T))
    lag = jnp.asarray(lag)
    sources = 2 * peers
    rows = sources * 16
    vmem = pl.BlockSpec(memory_space=pltpu.VMEM)
    hbm = pl.BlockSpec(memory_space=pl.ANY)
    b16, f32 = jnp.bfloat16, jnp.float32
    adj, misfit = pl.pallas_call(
        functools.partial(kernel, regions, peers, cap, local),
        out_shape=(
            jax.ShapeDtypeStruct((3 * local, ticks), b16),
            jax.ShapeDtypeStruct((1, pairs), f32),
        ),
        in_specs=[vmem] * 8 + [hbm] * 4,
        out_specs=(vmem, vmem),
        scratch_shapes=[
            pltpu.VMEM(w.shape, b16),
            pltpu.VMEM(wt.shape, b16),
            pltpu.VMEM(lag.shape, b16),
            pltpu.VMEM(lagt.shape, b16),
            pltpu.VMEM((cap, peers), jnp.int32),
            pltpu.VMEM((3, 4 * local, F), b16),
            pltpu.VMEM((3, sources, 16, F), b16),
            pltpu.VMEM((3, sources, 16, F), b16),
            pltpu.VMEM((3, sources, 16, BLOCK), b16),
            pltpu.VMEM((3, sources, 16, BLOCK), b16),
            pltpu.VMEM((3, local, 2 * F), b16),
            pltpu.VMEM((8 * pairs, rows), b16),
            pltpu.VMEM((rows, 8 * pairs), b16),
            pltpu.VMEM((rows, 64), b16),
            pltpu.VMEM((64, rows), b16),
            pltpu.VMEM((pairs, LAGS), f32),
            pltpu.VMEM((pairs, LAGS), f32),
            pltpu.VMEM((8 * pairs, BLOCK), b16),
            pltpu.SemaphoreType.DMA((4,)),
            pltpu.SemaphoreType.DMA((3,)),
            pltpu.SemaphoreType.DMA,
            pltpu.SemaphoreType.DMA,
            pltpu.SemaphoreType.DMA((3, sources)),
            pltpu.SemaphoreType.DMA((3, sources)),
            pltpu.SemaphoreType.DMA((3, sources)),
            pltpu.SemaphoreType.DMA((3, sources)),
        ],
        compiler_params=pltpu.CompilerParams(
            collective_id=0, has_side_effects=True, vmem_limit_bytes=60 * 1024 * 1024
        ),
    )(
        synthetic.transpose(1, 0, 2), observed.transpose(1, 0, 2), nearby.T, far_rows.T,
        first.reshape(1, pairs), second.reshape(1, pairs),
        start.reshape(1, pairs), length.reshape(1, pairs), w, wt, lag, lagt,
    )
    return adj.reshape(3, local, ticks).transpose(1, 0, 2), misfit.reshape(pairs)


def solution(mesh):
    placed = (P(("region", "dev"), None, None),) * 2 + (P(("region", "dev"), None),) * 2
    placed += (P(("region", "dev")),) * 4
    return jax.shard_map(
        functools.partial(on_device, mesh.shape["region"], mesh.shape["dev"]),
        mesh=mesh,
        in_specs=placed,
        out_specs=(P(("region", "dev"), None, None), P(("region", "dev"))),
        check_vma=False,
    )
```

```python
import functools
import math

import jax
import jax.numpy as jnp
import ml_dtypes
import numpy as np
from jax import lax
from jax.experimental import pallas as pl
from jax.experimental.pallas import tpu as pltpu
from jax.sharding import PartitionSpec as P

F = 512
FLOW = 64
LAGS = 512
BLOCK = 256
MESH = pl.DeviceIdType.MESH


def make_tables(ticks):
    rate = FLOW + np.arange(F, dtype=np.int64)
    angles = (np.arange(ticks)[:, None] * rate[None, :] % ticks) * (2.0 * math.pi / ticks)
    forward = np.concatenate([np.cos(angles), -np.sin(angles)], 1) / math.sqrt(ticks)
    shifts = np.arange(LAGS, dtype=np.int64) - LAGS // 2
    turning = (rate[:, None] * shifts[None, :] % ticks) * (2.0 * math.pi / ticks)
    lag = np.concatenate([np.cos(turning), -np.sin(turning)], 0) / math.sqrt(F)
    short = lambda x: x.astype(np.float32).astype(ml_dtypes.bfloat16)
    return short(forward), short(lag)


def dot(a, b):
    return jnp.dot(a, b, preferred_element_type=jnp.float32)


def one_hot(condition):
    return jnp.where(condition, 1.0, 0.0).astype(jnp.bfloat16)


def iota(shape, axis):
    return lax.broadcasted_iota(jnp.int32, shape, axis)


def down(row, width):
    pairs = row.shape[1]
    column = jnp.transpose(jnp.broadcast_to(row.astype(jnp.float32), (128, pairs)))
    return jnp.concatenate([column] * (width // 128), 1).astype(jnp.int32)


def kernel(
    regions, peers, cap, local,
    syn_ref, obs_ref, near_ref, far_ref, first_ref, second_ref, start_ref, length_ref,
    w_hbm, wt_hbm, lag_hbm, lagt_hbm,
    adj_ref, misfit_ref,
    w, wt, lag, lagt, far_in, sp, send, recv, gout, gin, own, pick, spread, sel_out, sel_in,
    inside, energy, grads,
    w_sem, table_sem, idx_send, idx_recv, send_sem, recv_sem, gsend_sem, grecv_sem,
):
    region, me = lax.axis_index("region"), lax.axis_index("dev")
    last = regions - 1
    sources = 2 * peers
    rows = sources * 16
    pairs = first_ref.shape[1]

    w_copies = [pltpu.make_async_copy(w_hbm.at[i], w.at[i], w_sem.at[i]) for i in range(4)]
    table_copies = [
        pltpu.make_async_copy(a, b, table_sem.at[i])
        for i, (a, b) in enumerate(((lag_hbm, lag), (lagt_hbm, lagt), (wt_hbm, wt)))
    ]
    for copy in w_copies + table_copies:
        copy.start()

    barrier = pltpu.get_barrier_semaphore()

    def greet(j, carry):
        @pl.when(j != me)
        def _():
            pl.semaphore_signal(barrier, inc=1, device_id=(region, j), device_id_type=MESH)

        @pl.when(region > 0)
        def _():
            pl.semaphore_signal(barrier, inc=1, device_id=(region - 1, j), device_id_type=MESH)

        @pl.when(region < last)
        def _():
            pl.semaphore_signal(barrier, inc=1, device_id=(region + 1, j), device_id_type=MESH)

        return carry

    lax.fori_loop(0, peers, greet, 0)
    below = jnp.where(region > 0, peers, 0)
    above = jnp.where(region < last, peers, 0)
    pl.semaphore_wait(barrier, peers - 1 + below + above)

    def idx_copy(target):
        return pltpu.make_async_remote_copy(
            src_ref=far_ref, dst_ref=far_in, send_sem=idx_send, recv_sem=idx_recv,
            device_id=(target, me), device_id_type=MESH,
        )

    @pl.when(region < last)
    def _():
        idx_copy(region + 1).start()

    @pl.when(region == 0)
    def _():
        far_in[...] = jnp.zeros_like(far_in)
        gin[:, peers:sources] = jnp.zeros((3, peers, 16, BLOCK), jnp.bfloat16)

    @pl.when(region == last)
    def _():
        recv[:, peers:sources] = jnp.zeros((3, peers, 16, F), jnp.bfloat16)

    count = 6 * local
    x = jnp.concatenate(
        [syn_ref[...].reshape(3 * local, -1), obs_ref[...].reshape(3 * local, -1)], 0
    ).astype(jnp.float32)
    middle = x.shape[1] // 2
    for half in range(2):
        x0, x1 = x[:, :middle], x[:, middle:]
        folded = x0 - x1 if half else x0 + x1
        high = folded.astype(jnp.bfloat16)
        low = (folded - high.astype(jnp.float32)).astype(jnp.bfloat16)
        both = jnp.concatenate([high, low], 0)
        for part in range(2):
            w_copies[half * 2 + part].wait()
            y = dot(both, w[half * 2 + part])
            y = (y[:count] + y[count:]).astype(jnp.bfloat16)
            for k in range(2):
                for c in range(3):
                    at = part * 32 + k * 16
                    sp[c, at : at + 16, half * BLOCK : (half + 1) * BLOCK] = y[
                        k * 48 + c * 16 : k * 48 + c * 16 + 16
                    ]

    @pl.when(region > 0)
    def _():
        idx_copy(region).wait_recv()

    near_owner = jnp.where(iota((peers, rows), 1) // 16 == iota((peers, rows), 0), 1.0, 0.0)
    far_owner = jnp.where(
        iota((peers, rows), 1) // 16 == iota((peers, rows), 0) + peers, 1.0, 0.0
    )
    wide = dot(near_ref[...].astype(jnp.float32), near_owner)
    wide += dot(far_in[...].astype(jnp.float32), far_owner)
    wide = jnp.where(iota((cap, rows), 1) % 4 == iota((cap, rows), 0), wide, 0.0)
    asked_row = jnp.broadcast_to(jnp.sum(wide, 0, keepdims=True), (128, rows))
    asked_col = jnp.transpose(asked_row)
    asked_row = asked_row[:64].astype(jnp.int32)
    row = iota((rows, 64), 0)
    column = (row // 4 % 2) * 32 + (row // 8 % 2) * 16 + asked_col[:, :64].astype(jnp.int32)
    sel_out[...] = one_hot(column == iota((rows, 64), 1))
    up = iota((64, rows), 0)
    sel_in[...] = one_hot((asked_row == up % 16) & (iota((64, rows), 1) // 4 % 4 == up // 16))

    def spectra_copy(c, to, src, dst, target):
        return pltpu.make_async_remote_copy(
            src_ref=send.at[c, src], dst_ref=recv.at[c, dst],
            send_sem=send_sem.at[c, src], recv_sem=recv_sem.at[c, dst],
            device_id=(to, target), device_id_type=MESH,
        )

    def grad_copy(c, to, src, dst, target):
        return pltpu.make_async_remote_copy(
            src_ref=gout.at[c, src], dst_ref=gin.at[c, dst],
            send_sem=gsend_sem.at[c, src], recv_sem=grecv_sem.at[c, dst],
            device_id=(to, target), device_id_type=MESH,
        )

    def exchange(c, carry):
        block = dot(sel_out[...], sp[c]).astype(jnp.bfloat16)
        send[c] = block.reshape(sources, 16, F)
        recv[c, me] = send[c, me]

        def go(i, carry):
            j = (me + 1 + i) % peers

            @pl.when(j != me)
            def _():
                spectra_copy(c, region, j, me, j).start()

            @pl.when(region > 0)
            def _():
                spectra_copy(c, region - 1, peers + j, peers + me, j).start()

            return carry

        return lax.fori_loop(0, peers, go, carry)

    lax.fori_loop(0, 3, exchange, 0)

    for end, ref in enumerate((first_ref, second_ref)):
        slot = ref[...]
        base = (slot >> 2) * 16 + (slot & 3)
        column = down(base, rows)
        lanes = iota((pairs, rows), 1)
        ups = iota((rows, pairs), 0)
        for o in range(4):
            at = (end * 4 + o) * pairs
            pick[at : at + pairs, :] = one_hot(lanes == column + 4 * o)
            spread[:, at : at + pairs] = one_hot(ups == base + 4 * o)
    position = iota((pairs, LAGS), 1)
    begin = down(start_ref[...], LAGS)
    stop = down(start_ref[...] + length_ref[...], LAGS)
    inside[...] = jnp.where((position >= begin) & (position < stop), 1.0, 0.0)
    energy[...] = jnp.zeros_like(energy)

    table_copies[0].wait()
    table_copies[1].wait()

    def work(c, carry):
        def arrive(j, carry):
            @pl.when(j != me)
            def _():
                spectra_copy(c, region, j, j, j).wait_recv()

            @pl.when(region < last)
            def _():
                spectra_copy(c, region, peers + j, peers + j, j).wait_recv()

            return carry

        lax.fori_loop(0, peers, arrive, 0)
        fetched = recv[c].reshape(rows, F)
        got = lambda end, o: dot(pick[(end * 4 + o) * pairs : (end * 4 + o + 1) * pairs], fetched)
        ar, ai, br, bi = got(0, 0), got(0, 1), got(1, 0), got(1, 1)
        ur, ui, vr, vi = got(0, 2), got(0, 3), got(1, 2), got(1, 3)
        change_re = ((ar * br + ai * bi) - (ur * vr + ui * vi)).astype(jnp.bfloat16)
        change_im = ((ai * br - ar * bi) - (ui * vr - ur * vi)).astype(jnp.bfloat16)
        shifted = dot(change_re, lag[:F]) + dot(change_im, lag[F:])
        residual = jnp.where(inside[...] > 0.5, shifted, 0.0)
        energy[...] += residual * residual
        short = residual.astype(jnp.bfloat16)
        gr, gi = dot(short, lagt[:, :F]), dot(short, lagt[:, F:])
        ends = (
            (gr * br - gi * bi, gr * bi + gi * br),
            (gr * ar + gi * ai, gr * ai - gi * ar),
        )
        for end in range(2):
            for part in range(2):
                value = ends[end][part].astype(jnp.bfloat16)
                for half in range(2):
                    at = (end * 4 + half * 2 + part) * pairs
                    grads[at : at + pairs] = value[:, half * BLOCK : (half + 1) * BLOCK]
        total = dot(spread[...], grads[...]).astype(jnp.bfloat16)
        gout[c] = total.reshape(sources, 16, BLOCK)
        gin[c, me] = gout[c, me]

        def go(i, carry):
            j = (me + 1 + i) % peers

            @pl.when(j != me)
            def _():
                grad_copy(c, region, j, me, j).start()

            @pl.when(region < last)
            def _():
                grad_copy(c, region + 1, peers + j, peers + me, j).start()

            return carry

        return lax.fori_loop(0, peers, go, carry)

    lax.fori_loop(0, 3, work, 0)

    power = energy[:, :128]
    for i in range(1, LAGS // 128):
        power = power + energy[:, i * 128 : (i + 1) * 128]
    misfit_ref[...] = jnp.sum(jnp.transpose(power), 0, keepdims=True) / (2.0 * LAGS)

    def settle(c, carry):
        def arrive(j, carry):
            @pl.when(j != me)
            def _():
                grad_copy(c, region, j, j, j).wait_recv()

            @pl.when(region > 0)
            def _():
                grad_copy(c, region, peers + j, peers + j, j).wait_recv()

            return carry

        lax.fori_loop(0, peers, arrive, 0)
        total = dot(sel_in[...], gin[c].reshape(rows, BLOCK)).astype(jnp.bfloat16)
        for half in range(2):
            for part in range(2):
                o = half * 2 + part
                own[half, c, :, part * BLOCK : (part + 1) * BLOCK] = total[o * 16 : o * 16 + 16]
        return carry

    lax.fori_loop(0, 3, settle, 0)

    table_copies[2].wait()
    even = own[0].reshape(3 * local, F)
    odd = own[1].reshape(3 * local, F)
    width = wt.shape[3]

    def back(i, carry):
        at = pl.multiple_of(i * width, width)
        plain, signed = dot(even, wt[i, 0]), dot(odd, wt[i, 1])
        adj_ref[:, pl.ds(at, width)] = (plain + signed).astype(jnp.bfloat16)
        adj_ref[:, pl.ds(at + middle, width)] = (plain - signed).astype(jnp.bfloat16)
        return carry

    lax.fori_loop(0, wt.shape[0], back, 0)

    def sent(i, carry):
        c, j = i // peers, i % peers

        @pl.when(j != me)
        def _():
            spectra_copy(c, region, j, j, j).wait_send()
            grad_copy(c, region, j, j, j).wait_send()

        @pl.when(region > 0)
        def _():
            spectra_copy(c, region, peers + j, peers + j, j).wait_send()

        @pl.when(region < last)
        def _():
            grad_copy(c, region, peers + j, peers + j, j).wait_send()

        return carry

    lax.fori_loop(0, 3 * peers, sent, 0)

    @pl.when(region < last)
    def _():
        idx_copy(region).wait_send()


def on_device(
    regions, peers, synthetic, observed, nearby, far_rows, first, second, start, length
):
    local, _, ticks = synthetic.shape
    cap = nearby.shape[1]
    pairs = first.shape[0]
    forward, lag = make_tables(ticks)
    middle, width = ticks // 2, 512
    forward = forward[:middle].reshape(middle, 2, F // 2, 2).transpose(3, 1, 2, 0)
    lag = lag.reshape(2, F // 2, 2, LAGS).transpose(0, 2, 1, 3).reshape(2 * F, LAGS)
    plain = lambda a: jnp.asarray(np.ascontiguousarray(a))
    w = plain(forward.reshape(4, BLOCK, middle).transpose(0, 2, 1))
    wt = plain(forward.reshape(2, F, middle // width, width).transpose(2, 0, 1, 3))
    lagt = plain(lag.T)
    lag = plain(lag)
    sources = 2 * peers
    rows = sources * 16
    vmem = pl.BlockSpec(memory_space=pltpu.VMEM)
    hbm = pl.BlockSpec(memory_space=pl.ANY)
    b16, f32 = jnp.bfloat16, jnp.float32
    adj, misfit = pl.pallas_call(
        functools.partial(kernel, regions, peers, cap, local),
        out_shape=(
            jax.ShapeDtypeStruct((3 * local, ticks), b16),
            jax.ShapeDtypeStruct((1, pairs), f32),
        ),
        in_specs=[vmem] * 8 + [hbm] * 4,
        out_specs=(vmem, vmem),
        scratch_shapes=[
            pltpu.VMEM(w.shape, b16),
            pltpu.VMEM(wt.shape, b16),
            pltpu.VMEM(lag.shape, b16),
            pltpu.VMEM(lagt.shape, b16),
            pltpu.VMEM((cap, peers), jnp.int32),
            pltpu.VMEM((3, 4 * local, F), b16),
            pltpu.VMEM((3, sources, 16, F), b16),
            pltpu.VMEM((3, sources, 16, F), b16),
            pltpu.VMEM((3, sources, 16, BLOCK), b16),
            pltpu.VMEM((3, sources, 16, BLOCK), b16),
            pltpu.VMEM((2, 3, local, F), b16),
            pltpu.VMEM((8 * pairs, rows), b16),
            pltpu.VMEM((rows, 8 * pairs), b16),
            pltpu.VMEM((rows, 64), b16),
            pltpu.VMEM((64, rows), b16),
            pltpu.VMEM((pairs, LAGS), f32),
            pltpu.VMEM((pairs, LAGS), f32),
            pltpu.VMEM((8 * pairs, BLOCK), b16),
            pltpu.SemaphoreType.DMA((4,)),
            pltpu.SemaphoreType.DMA((3,)),
            pltpu.SemaphoreType.DMA,
            pltpu.SemaphoreType.DMA,
            pltpu.SemaphoreType.DMA((3, sources)),
            pltpu.SemaphoreType.DMA((3, sources)),
            pltpu.SemaphoreType.DMA((3, sources)),
            pltpu.SemaphoreType.DMA((3, sources)),
        ],
        compiler_params=pltpu.CompilerParams(
            collective_id=0, has_side_effects=True, vmem_limit_bytes=60 * 1024 * 1024
        ),
    )(
        synthetic.transpose(1, 0, 2), observed.transpose(1, 0, 2), nearby.T, far_rows.T,
        first.reshape(1, pairs), second.reshape(1, pairs),
        start.reshape(1, pairs), length.reshape(1, pairs), w, wt, lag, lagt,
    )
    return adj.reshape(3, local, ticks).transpose(1, 0, 2), misfit.reshape(pairs)


def solution(mesh):
    placed = (P(("region", "dev"), None, None),) * 2 + (P(("region", "dev"), None),) * 2
    placed += (P(("region", "dev")),) * 4
    return jax.shard_map(
        functools.partial(on_device, mesh.shape["region"], mesh.shape["dev"]),
        mesh=mesh,
        in_specs=placed,
        out_specs=(P(("region", "dev"), None, None), P(("region", "dev"))),
        check_vma=False,
    )
```

```python
import functools
import math

import jax
import jax.numpy as jnp
import ml_dtypes
import numpy as np
from jax import lax
from jax.experimental import pallas as pl
from jax.experimental.pallas import tpu as pltpu
from jax.sharding import PartitionSpec as P

F = 512
FLOW = 64
LAGS = 512
BLOCK = 256
MESH = pl.DeviceIdType.MESH


def make_tables(ticks):
    rate = FLOW + np.arange(F, dtype=np.int64)
    angles = (np.arange(ticks)[:, None] * rate[None, :] % ticks) * (2.0 * math.pi / ticks)
    forward = np.concatenate([np.cos(angles), -np.sin(angles)], 1) / math.sqrt(ticks)
    shifts = np.arange(LAGS, dtype=np.int64) - LAGS // 2
    turning = (rate[:, None] * shifts[None, :] % ticks) * (2.0 * math.pi / ticks)
    lag = np.concatenate([np.cos(turning), -np.sin(turning)], 0) / math.sqrt(F)
    short = lambda x: x.astype(np.float32).astype(ml_dtypes.bfloat16)
    return short(forward), short(lag)


def dot(a, b):
    return jnp.dot(a, b, preferred_element_type=jnp.float32)


def one_hot(condition):
    return jnp.where(condition, 1.0, 0.0).astype(jnp.bfloat16)


def iota(shape, axis):
    return lax.broadcasted_iota(jnp.int32, shape, axis)


def down(row, width):
    pairs = row.shape[1]
    column = jnp.transpose(jnp.broadcast_to(row.astype(jnp.float32), (128, pairs)))
    return jnp.concatenate([column] * (width // 128), 1).astype(jnp.int32)


def kernel(
    regions, peers, cap, local,
    syn_ref, obs_ref, near_ref, far_ref, first_ref, second_ref, start_ref, length_ref,
    w_hbm, wt_hbm, lag_hbm, lagt_hbm,
    adj_ref, misfit_ref,
    w, wt, lag, lagt, far_in, sp, send, recv, gout, gin, own, pick, spread, sel_out, sel_in,
    inside, energy, grads,
    w_sem, table_sem, idx_send, idx_recv, send_sem, recv_sem, gsend_sem, grecv_sem,
):
    region, me = lax.axis_index("region"), lax.axis_index("dev")
    last = regions - 1
    sources = 2 * peers
    rows = sources * 16
    pairs = first_ref.shape[1]

    w_copies = [pltpu.make_async_copy(w_hbm.at[i], w.at[i], w_sem.at[i]) for i in range(4)]
    table_copies = [
        pltpu.make_async_copy(a, b, table_sem.at[i])
        for i, (a, b) in enumerate(((lag_hbm, lag), (lagt_hbm, lagt), (wt_hbm, wt)))
    ]
    for copy in w_copies + table_copies:
        copy.start()

    barrier = pltpu.get_barrier_semaphore()

    def greet(j, carry):
        @pl.when(j != me)
        def _():
            pl.semaphore_signal(barrier, inc=1, device_id=(region, j), device_id_type=MESH)

        @pl.when(region > 0)
        def _():
            pl.semaphore_signal(barrier, inc=1, device_id=(region - 1, j), device_id_type=MESH)

        @pl.when(region < last)
        def _():
            pl.semaphore_signal(barrier, inc=1, device_id=(region + 1, j), device_id_type=MESH)

        return carry

    lax.fori_loop(0, peers, greet, 0)
    below = jnp.where(region > 0, peers, 0)
    above = jnp.where(region < last, peers, 0)
    pl.semaphore_wait(barrier, peers - 1 + below + above)

    def idx_copy(target):
        return pltpu.make_async_remote_copy(
            src_ref=far_ref, dst_ref=far_in, send_sem=idx_send, recv_sem=idx_recv,
            device_id=(target, me), device_id_type=MESH,
        )

    @pl.when(region < last)
    def _():
        idx_copy(region + 1).start()

    @pl.when(region == 0)
    def _():
        far_in[...] = jnp.zeros_like(far_in)
        gin[:, peers:sources] = jnp.zeros((3, peers, 16, BLOCK), jnp.bfloat16)

    @pl.when(region == last)
    def _():
        recv[:, peers:sources] = jnp.zeros((3, peers, 16, F), jnp.bfloat16)

    count = 6 * local
    x = jnp.concatenate(
        [syn_ref[...].reshape(3 * local, -1), obs_ref[...].reshape(3 * local, -1)], 0
    ).astype(jnp.float32)
    middle = x.shape[1] // 2
    for half in range(2):
        x0, x1 = x[:, :middle], x[:, middle:]
        folded = x0 - x1 if half else x0 + x1
        high = folded.astype(jnp.bfloat16)
        low = (folded - high.astype(jnp.float32)).astype(jnp.bfloat16)
        both = jnp.concatenate([high, low], 0)
        for part in range(2):
            w_copies[half * 2 + part].wait()
            y = dot(both, w[half * 2 + part])
            y = (y[:count] + y[count:]).astype(jnp.bfloat16)
            for k in range(2):
                for c in range(3):
                    at = part * 32 + k * 16
                    sp[c, at : at + 16, half * BLOCK : (half + 1) * BLOCK] = y[
                        k * 48 + c * 16 : k * 48 + c * 16 + 16
                    ]

    @pl.when(region > 0)
    def _():
        idx_copy(region).wait_recv()

    near_owner = jnp.where(iota((peers, rows), 1) // 16 == iota((peers, rows), 0), 1.0, 0.0)
    far_owner = jnp.where(
        iota((peers, rows), 1) // 16 == iota((peers, rows), 0) + peers, 1.0, 0.0
    )
    wide = dot(near_ref[...].astype(jnp.float32), near_owner)
    wide += dot(far_in[...].astype(jnp.float32), far_owner)
    wide = jnp.where(iota((cap, rows), 1) % 4 == iota((cap, rows), 0), wide, 0.0)
    asked_row = jnp.broadcast_to(jnp.sum(wide, 0, keepdims=True), (128, rows))
    asked_col = jnp.transpose(asked_row)
    asked_row = asked_row[:64].astype(jnp.int32)
    row = iota((rows, 64), 0)
    column = (row // 4 % 2) * 32 + (row // 8 % 2) * 16 + asked_col[:, :64].astype(jnp.int32)
    sel_out[...] = one_hot(column == iota((rows, 64), 1))
    up = iota((64, rows), 0)
    sel_in[...] = one_hot((asked_row == up % 16) & (iota((64, rows), 1) // 4 % 4 == up // 16))

    def spectra_copy(c, to, src, dst, target):
        return pltpu.make_async_remote_copy(
            src_ref=send.at[c, src], dst_ref=recv.at[c, dst],
            send_sem=send_sem.at[c, src], recv_sem=recv_sem.at[c, dst],
            device_id=(to, target), device_id_type=MESH,
        )

    def grad_copy(c, to, src, dst, target):
        return pltpu.make_async_remote_copy(
            src_ref=gout.at[c, src], dst_ref=gin.at[c, dst],
            send_sem=gsend_sem.at[c, src], recv_sem=grecv_sem.at[c, dst],
            device_id=(to, target), device_id_type=MESH,
        )

    def exchange(c, carry):
        block = dot(sel_out[...], sp[c]).astype(jnp.bfloat16)
        send[c] = block.reshape(sources, 16, F)
        recv[c, me] = send[c, me]

        def go(i, carry):
            j = (me + 1 + i) % peers

            @pl.when(j != me)
            def _():
                spectra_copy(c, region, j, me, j).start()

            @pl.when(region > 0)
            def _():
                spectra_copy(c, region - 1, peers + j, peers + me, j).start()

            return carry

        return lax.fori_loop(0, peers, go, carry)

    lax.fori_loop(0, 2, exchange, 0)

    for end, ref in enumerate((first_ref, second_ref)):
        slot = ref[...]
        base = (slot >> 2) * 16 + (slot & 3)
        column = down(base, rows)
        lanes = iota((pairs, rows), 1)
        ups = iota((rows, pairs), 0)
        for o in range(4):
            at = (end * 4 + o) * pairs
            pick[at : at + pairs, :] = one_hot(lanes == column + 4 * o)
            spread[:, at : at + pairs] = one_hot(ups == base + 4 * o)
    position = iota((pairs, LAGS), 1)
    begin = down(start_ref[...], LAGS)
    stop = down(start_ref[...] + length_ref[...], LAGS)
    inside[...] = jnp.where((position >= begin) & (position < stop), 1.0, 0.0)
    energy[...] = jnp.zeros_like(energy)

    table_copies[0].wait()
    table_copies[1].wait()

    def work(c, carry):
        def arrive(j, carry):
            @pl.when(j != me)
            def _():
                spectra_copy(c, region, j, j, j).wait_recv()

            @pl.when(region < last)
            def _():
                spectra_copy(c, region, peers + j, peers + j, j).wait_recv()

            return carry

        lax.fori_loop(0, peers, arrive, 0)

        @pl.when(c == 0)
        def _():
            exchange(2, 0)

        fetched = recv[c].reshape(rows, F)
        got = lambda end, o: dot(pick[(end * 4 + o) * pairs : (end * 4 + o + 1) * pairs], fetched)
        ar, ai, br, bi = got(0, 0), got(0, 1), got(1, 0), got(1, 1)
        ur, ui, vr, vi = got(0, 2), got(0, 3), got(1, 2), got(1, 3)
        change_re = ((ar * br + ai * bi) - (ur * vr + ui * vi)).astype(jnp.bfloat16)
        change_im = ((ai * br - ar * bi) - (ui * vr - ur * vi)).astype(jnp.bfloat16)
        shifted = dot(change_re, lag[:F]) + dot(change_im, lag[F:])
        residual = jnp.where(inside[...] > 0.5, shifted, 0.0)
        energy[...] += residual * residual
        short = residual.astype(jnp.bfloat16)
        gr, gi = dot(short, lagt[:, :F]), dot(short, lagt[:, F:])
        ends = (
            (gr * br - gi * bi, gr * bi + gi * br),
            (gr * ar + gi * ai, gr * ai - gi * ar),
        )
        for end in range(2):
            for part in range(2):
                value = ends[end][part].astype(jnp.bfloat16)
                for half in range(2):
                    at = (end * 4 + half * 2 + part) * pairs
                    grads[at : at + pairs] = value[:, half * BLOCK : (half + 1) * BLOCK]
        total = dot(spread[...], grads[...]).astype(jnp.bfloat16)
        gout[c] = total.reshape(sources, 16, BLOCK)
        gin[c, me] = gout[c, me]

        def go(i, carry):
            j = (me + 1 + i) % peers

            @pl.when(j != me)
            def _():
                grad_copy(c, region, j, me, j).start()

            @pl.when(region < last)
            def _():
                grad_copy(c, region + 1, peers + j, peers + me, j).start()

            return carry

        return lax.fori_loop(0, peers, go, carry)

    lax.fori_loop(0, 3, work, 0)

    power = energy[:, :128]
    for i in range(1, LAGS // 128):
        power = power + energy[:, i * 128 : (i + 1) * 128]
    misfit_ref[...] = jnp.sum(jnp.transpose(power), 0, keepdims=True) / (2.0 * LAGS)

    def settle(c, carry):
        def arrive(j, carry):
            @pl.when(j != me)
            def _():
                grad_copy(c, region, j, j, j).wait_recv()

            @pl.when(region > 0)
            def _():
                grad_copy(c, region, peers + j, peers + j, j).wait_recv()

            return carry

        lax.fori_loop(0, peers, arrive, 0)
        total = dot(sel_in[...], gin[c].reshape(rows, BLOCK)).astype(jnp.bfloat16)
        for half in range(2):
            for part in range(2):
                o = half * 2 + part
                own[half, c, :, part * BLOCK : (part + 1) * BLOCK] = total[o * 16 : o * 16 + 16]
        return carry

    lax.fori_loop(0, 3, settle, 0)

    table_copies[2].wait()
    even = own[0].reshape(3 * local, F)
    odd = own[1].reshape(3 * local, F)
    width = wt.shape[3]

    def back(i, carry):
        at = pl.multiple_of(i * width, width)
        plain, signed = dot(even, wt[i, 0]), dot(odd, wt[i, 1])
        adj_ref[:, pl.ds(at, width)] = (plain + signed).astype(jnp.bfloat16)
        adj_ref[:, pl.ds(at + middle, width)] = (plain - signed).astype(jnp.bfloat16)
        return carry

    lax.fori_loop(0, wt.shape[0], back, 0)

    def sent(i, carry):
        c, j = i // peers, i % peers

        @pl.when(j != me)
        def _():
            spectra_copy(c, region, j, j, j).wait_send()
            grad_copy(c, region, j, j, j).wait_send()

        @pl.when(region > 0)
        def _():
            spectra_copy(c, region, peers + j, peers + j, j).wait_send()

        @pl.when(region < last)
        def _():
            grad_copy(c, region, peers + j, peers + j, j).wait_send()

        return carry

    lax.fori_loop(0, 3 * peers, sent, 0)

    @pl.when(region < last)
    def _():
        idx_copy(region).wait_send()


def on_device(
    regions, peers, synthetic, observed, nearby, far_rows, first, second, start, length
):
    local, _, ticks = synthetic.shape
    cap = nearby.shape[1]
    pairs = first.shape[0]
    forward, lag = make_tables(ticks)
    middle, width = ticks // 2, 512
    forward = forward[:middle].reshape(middle, 2, F // 2, 2).transpose(3, 1, 2, 0)
    lag = lag.reshape(2, F // 2, 2, LAGS).transpose(0, 2, 1, 3).reshape(2 * F, LAGS)
    plain = lambda a: jnp.asarray(np.ascontiguousarray(a))
    w = plain(forward.reshape(4, BLOCK, middle).transpose(0, 2, 1))
    wt = plain(forward.reshape(2, F, middle // width, width).transpose(2, 0, 1, 3))
    lagt = plain(lag.T)
    lag = plain(lag)
    sources = 2 * peers
    rows = sources * 16
    vmem = pl.BlockSpec(memory_space=pltpu.VMEM)
    hbm = pl.BlockSpec(memory_space=pl.ANY)
    b16, f32 = jnp.bfloat16, jnp.float32
    adj, misfit = pl.pallas_call(
        functools.partial(kernel, regions, peers, cap, local),
        out_shape=(
            jax.ShapeDtypeStruct((3 * local, ticks), b16),
            jax.ShapeDtypeStruct((1, pairs), f32),
        ),
        in_specs=[vmem] * 8 + [hbm] * 4,
        out_specs=(vmem, vmem),
        scratch_shapes=[
            pltpu.VMEM(w.shape, b16),
            pltpu.VMEM(wt.shape, b16),
            pltpu.VMEM(lag.shape, b16),
            pltpu.VMEM(lagt.shape, b16),
            pltpu.VMEM((cap, peers), jnp.int32),
            pltpu.VMEM((3, 4 * local, F), b16),
            pltpu.VMEM((3, sources, 16, F), b16),
            pltpu.VMEM((3, sources, 16, F), b16),
            pltpu.VMEM((3, sources, 16, BLOCK), b16),
            pltpu.VMEM((3, sources, 16, BLOCK), b16),
            pltpu.VMEM((2, 3, local, F), b16),
            pltpu.VMEM((8 * pairs, rows), b16),
            pltpu.VMEM((rows, 8 * pairs), b16),
            pltpu.VMEM((rows, 64), b16),
            pltpu.VMEM((64, rows), b16),
            pltpu.VMEM((pairs, LAGS), f32),
            pltpu.VMEM((pairs, LAGS), f32),
            pltpu.VMEM((8 * pairs, BLOCK), b16),
            pltpu.SemaphoreType.DMA((4,)),
            pltpu.SemaphoreType.DMA((3,)),
            pltpu.SemaphoreType.DMA,
            pltpu.SemaphoreType.DMA,
            pltpu.SemaphoreType.DMA((3, sources)),
            pltpu.SemaphoreType.DMA((3, sources)),
            pltpu.SemaphoreType.DMA((3, sources)),
            pltpu.SemaphoreType.DMA((3, sources)),
        ],
        compiler_params=pltpu.CompilerParams(
            collective_id=0, has_side_effects=True, vmem_limit_bytes=60 * 1024 * 1024
        ),
    )(
        synthetic.transpose(1, 0, 2), observed.transpose(1, 0, 2), nearby.T, far_rows.T,
        first.reshape(1, pairs), second.reshape(1, pairs),
        start.reshape(1, pairs), length.reshape(1, pairs), w, wt, lag, lagt,
    )
    return adj.reshape(3, local, ticks).transpose(1, 0, 2), misfit.reshape(pairs)


def solution(mesh):
    placed = (P(("region", "dev"), None, None),) * 2 + (P(("region", "dev"), None),) * 2
    placed += (P(("region", "dev")),) * 4
    return jax.shard_map(
        functools.partial(on_device, mesh.shape["region"], mesh.shape["dev"]),
        mesh=mesh,
        in_specs=placed,
        out_specs=(P(("region", "dev"), None, None), P(("region", "dev"))),
        check_vma=False,
    )
```

```python
import functools
import math

import jax
import jax.numpy as jnp
import ml_dtypes
import numpy as np
from jax import lax
from jax.experimental import pallas as pl
from jax.experimental.pallas import tpu as pltpu
from jax.sharding import PartitionSpec as P

F = 512
FLOW = 64
LAGS = 512
BLOCK = 256
MESH = pl.DeviceIdType.MESH


def make_tables(ticks):
    rate = FLOW + np.arange(F, dtype=np.int64)
    angles = (np.arange(ticks)[:, None] * rate[None, :] % ticks) * (2.0 * math.pi / ticks)
    forward = np.concatenate([np.cos(angles), -np.sin(angles)], 1) / math.sqrt(ticks)
    shifts = np.arange(LAGS, dtype=np.int64) - LAGS // 2
    turning = (rate[:, None] * shifts[None, :] % ticks) * (2.0 * math.pi / ticks)
    lag = np.concatenate([np.cos(turning), -np.sin(turning)], 0) / math.sqrt(F)
    short = lambda x: x.astype(np.float32).astype(ml_dtypes.bfloat16)
    return short(forward), short(lag)


def dot(a, b):
    return jnp.dot(a, b, preferred_element_type=jnp.float32)


def one_hot(condition):
    return jnp.where(condition, 1.0, 0.0).astype(jnp.bfloat16)


def iota(shape, axis):
    return lax.broadcasted_iota(jnp.int32, shape, axis)


def down(row, width):
    pairs = row.shape[1]
    column = jnp.transpose(jnp.broadcast_to(row.astype(jnp.float32), (128, pairs)))
    return jnp.concatenate([column] * (width // 128), 1).astype(jnp.int32)


def kernel(
    regions, peers, cap, local,
    syn_ref, obs_ref, near_ref, far_ref, first_ref, second_ref, start_ref, length_ref,
    w_hbm, wt_hbm, lag_hbm, lagt_hbm,
    adj_ref, misfit_ref,
    w, wt, lag, lagt, far_in, sp, send, recv, gout, gin, own, pick, spread, sel_out, sel_in,
    inside, energy, grads, got, change, slope,
    w_sem, table_sem, idx_send, idx_recv, send_sem, recv_sem, gsend_sem, grecv_sem,
):
    region, me = lax.axis_index("region"), lax.axis_index("dev")
    last = regions - 1
    sources = 2 * peers
    rows = sources * 16
    pairs = first_ref.shape[1]

    w_copies = [pltpu.make_async_copy(w_hbm.at[i], w.at[i], w_sem.at[i]) for i in range(4)]
    table_copies = [
        pltpu.make_async_copy(a, b, table_sem.at[i])
        for i, (a, b) in enumerate(((lag_hbm, lag), (lagt_hbm, lagt), (wt_hbm, wt)))
    ]
    for copy in w_copies + table_copies:
        copy.start()

    barrier = pltpu.get_barrier_semaphore()

    def greet(j, carry):
        @pl.when(j != me)
        def _():
            pl.semaphore_signal(barrier, inc=1, device_id=(region, j), device_id_type=MESH)

        @pl.when(region > 0)
        def _():
            pl.semaphore_signal(barrier, inc=1, device_id=(region - 1, j), device_id_type=MESH)

        @pl.when(region < last)
        def _():
            pl.semaphore_signal(barrier, inc=1, device_id=(region + 1, j), device_id_type=MESH)

        return carry

    lax.fori_loop(0, peers, greet, 0)
    below = jnp.where(region > 0, peers, 0)
    above = jnp.where(region < last, peers, 0)
    pl.semaphore_wait(barrier, peers - 1 + below + above)

    def idx_copy(target):
        return pltpu.make_async_remote_copy(
            src_ref=far_ref, dst_ref=far_in, send_sem=idx_send, recv_sem=idx_recv,
            device_id=(target, me), device_id_type=MESH,
        )

    @pl.when(region < last)
    def _():
        idx_copy(region + 1).start()

    @pl.when(region == 0)
    def _():
        far_in[...] = jnp.zeros_like(far_in)
        gin[:, peers:sources] = jnp.zeros((3, peers, 16, BLOCK), jnp.bfloat16)

    @pl.when(region == last)
    def _():
        recv[:, peers:sources] = jnp.zeros((3, peers, 16, F), jnp.bfloat16)

    count = 6 * local
    x = jnp.concatenate(
        [syn_ref[...].reshape(3 * local, -1), obs_ref[...].reshape(3 * local, -1)], 0
    ).astype(jnp.float32)
    middle = x.shape[1] // 2
    for half in range(2):
        x0, x1 = x[:, :middle], x[:, middle:]
        folded = x0 - x1 if half else x0 + x1
        high = folded.astype(jnp.bfloat16)
        low = (folded - high.astype(jnp.float32)).astype(jnp.bfloat16)
        both = jnp.concatenate([high, low], 0)
        for part in range(2):
            w_copies[half * 2 + part].wait()
            y = dot(both, w[half * 2 + part])
            y = (y[:count] + y[count:]).astype(jnp.bfloat16)
            for k in range(2):
                for c in range(3):
                    at = part * 32 + k * 16
                    sp[c, at : at + 16, half * BLOCK : (half + 1) * BLOCK] = y[
                        k * 48 + c * 16 : k * 48 + c * 16 + 16
                    ]

    @pl.when(region > 0)
    def _():
        idx_copy(region).wait_recv()

    near_owner = jnp.where(iota((peers, rows), 1) // 16 == iota((peers, rows), 0), 1.0, 0.0)
    far_owner = jnp.where(
        iota((peers, rows), 1) // 16 == iota((peers, rows), 0) + peers, 1.0, 0.0
    )
    wide = dot(near_ref[...].astype(jnp.float32), near_owner)
    wide += dot(far_in[...].astype(jnp.float32), far_owner)
    wide = jnp.where(iota((cap, rows), 1) % 4 == iota((cap, rows), 0), wide, 0.0)
    asked_row = jnp.broadcast_to(jnp.sum(wide, 0, keepdims=True), (128, rows))
    asked_col = jnp.transpose(asked_row)
    asked_row = asked_row[:64].astype(jnp.int32)
    row = iota((rows, 64), 0)
    column = (row // 4 % 2) * 32 + (row // 8 % 2) * 16 + asked_col[:, :64].astype(jnp.int32)
    sel_out[...] = one_hot(column == iota((rows, 64), 1))
    up = iota((64, rows), 0)
    sel_in[...] = one_hot((asked_row == up % 16) & (iota((64, rows), 1) // 4 % 4 == up // 16))

    def spectra_copy(c, to, src, dst, target):
        return pltpu.make_async_remote_copy(
            src_ref=send.at[c, src], dst_ref=recv.at[c, dst],
            send_sem=send_sem.at[c, src], recv_sem=recv_sem.at[c, dst],
            device_id=(to, target), device_id_type=MESH,
        )

    def grad_copy(c, to, src, dst, target):
        return pltpu.make_async_remote_copy(
            src_ref=gout.at[c, src], dst_ref=gin.at[c, dst],
            send_sem=gsend_sem.at[c, src], recv_sem=grecv_sem.at[c, dst],
            device_id=(to, target), device_id_type=MESH,
        )

    def exchange(c, carry):
        block = dot(sel_out[...], sp[c]).astype(jnp.bfloat16)
        send[c] = block.reshape(sources, 16, F)
        recv[c, me] = send[c, me]

        def go(i, carry):
            j = (me + 1 + i) % peers

            @pl.when(j != me)
            def _():
                spectra_copy(c, region, j, me, j).start()

            @pl.when(region > 0)
            def _():
                spectra_copy(c, region - 1, peers + j, peers + me, j).start()

            return carry

        return lax.fori_loop(0, peers, go, carry)

    lax.fori_loop(0, 3, exchange, 0)

    for end, ref in enumerate((first_ref, second_ref)):
        slot = ref[...]
        base = (slot >> 2) * 16 + (slot & 3)
        column = down(base, rows)
        lanes = iota((pairs, rows), 1)
        ups = iota((rows, pairs), 0)
        for o in range(4):
            at = (end * 4 + o) * pairs
            pick[at : at + pairs, :] = one_hot(lanes == column + 4 * o)
            spread[:, at : at + pairs] = one_hot(ups == base + 4 * o)
    position = iota((pairs, LAGS), 1)
    begin = down(start_ref[...], LAGS)
    stop = down(start_ref[...] + length_ref[...], LAGS)
    inside[...] = jnp.where((position >= begin) & (position < stop), 1.0, 0.0)
    energy[...] = jnp.zeros_like(energy)

    table_copies[0].wait()
    table_copies[1].wait()

    def work(c, carry):
        def arrive(j, carry):
            @pl.when(j != me)
            def _():
                spectra_copy(c, region, j, j, j).wait_recv()

            @pl.when(region < last)
            def _():
                spectra_copy(c, region, peers + j, peers + j, j).wait_recv()

            return carry

        lax.fori_loop(0, peers, arrive, 0)
        fetched = recv[c].reshape(rows, F)
        for v in range(8):
            got[v] = dot(pick[v * pairs : (v + 1) * pairs], fetched).astype(jnp.bfloat16)
        halves = [pl.ds(half * BLOCK, BLOCK) for half in range(2)]
        imaginary = [pl.ds(F + half * BLOCK, BLOCK) for half in range(2)]

        def cross(i, carry):
            at = pl.ds(pl.multiple_of(i * 16, 16), 16)
            for half in range(2):
                ar, ai, ur, ui, br, bi, vr, vi = [
                    got[v, at, halves[half]].astype(jnp.float32) for v in range(8)
                ]
                change_re = (ar * br + ai * bi) - (ur * vr + ui * vi)
                change_im = (ai * br - ar * bi) - (ui * vr - ur * vi)
                change[at, halves[half]] = change_re.astype(jnp.bfloat16)
                change[at, imaginary[half]] = change_im.astype(jnp.bfloat16)
            return carry

        lax.fori_loop(0, pairs // 16, cross, 0, unroll=2)
        shifted = dot(change[...], lag[...])
        residual = shifted * inside[...]
        energy[...] += residual * residual
        slope[...] = dot(residual.astype(jnp.bfloat16), lagt[...])

        def chain(i, carry):
            at = pl.ds(pl.multiple_of(i * 16, 16), 16)
            for half in range(2):
                gr, gi = slope[at, halves[half]], slope[at, imaginary[half]]
                ar, ai, br, bi = [
                    got[v, at, halves[half]].astype(jnp.float32) for v in (0, 1, 4, 5)
                ]
                values = (
                    gr * br - gi * bi, gr * bi + gi * br, gr * ar + gi * ai, gr * ai - gi * ar
                )
                for j in range(4):
                    start = (j // 2 * 4 + half * 2 + j % 2) * pairs
                    rows_at = pl.ds(pl.multiple_of(start + i * 16, 16), 16)
                    grads[rows_at] = values[j].astype(jnp.bfloat16)
            return carry

        lax.fori_loop(0, pairs // 16, chain, 0, unroll=2)
        total = dot(spread[...], grads[...]).astype(jnp.bfloat16)
        gout[c] = total.reshape(sources, 16, BLOCK)
        gin[c, me] = gout[c, me]

        def go(i, carry):
            j = (me + 1 + i) % peers

            @pl.when(j != me)
            def _():
                grad_copy(c, region, j, me, j).start()

            @pl.when(region < last)
            def _():
                grad_copy(c, region + 1, peers + j, peers + me, j).start()

            return carry

        return lax.fori_loop(0, peers, go, carry)

    lax.fori_loop(0, 3, work, 0)

    power = energy[:, :128]
    for i in range(1, LAGS // 128):
        power = power + energy[:, i * 128 : (i + 1) * 128]
    misfit_ref[...] = jnp.sum(jnp.transpose(power), 0, keepdims=True) / (2.0 * LAGS)

    def settle(c, carry):
        def arrive(j, carry):
            @pl.when(j != me)
            def _():
                grad_copy(c, region, j, j, j).wait_recv()

            @pl.when(region > 0)
            def _():
                grad_copy(c, region, peers + j, peers + j, j).wait_recv()

            return carry

        lax.fori_loop(0, peers, arrive, 0)
        total = dot(sel_in[...], gin[c].reshape(rows, BLOCK)).astype(jnp.bfloat16)
        for half in range(2):
            for part in range(2):
                o = half * 2 + part
                own[half, c, :, part * BLOCK : (part + 1) * BLOCK] = total[o * 16 : o * 16 + 16]
        return carry

    lax.fori_loop(0, 3, settle, 0)

    table_copies[2].wait()
    even = own[0].reshape(3 * local, F)
    odd = own[1].reshape(3 * local, F)
    width = wt.shape[3]

    def back(i, carry):
        at = pl.multiple_of(i * width, width)
        plain, signed = dot(even, wt[i, 0]), dot(odd, wt[i, 1])
        adj_ref[:, pl.ds(at, width)] = (plain + signed).astype(jnp.bfloat16)
        adj_ref[:, pl.ds(at + middle, width)] = (plain - signed).astype(jnp.bfloat16)
        return carry

    lax.fori_loop(0, wt.shape[0], back, 0)

    def sent(i, carry):
        c, j = i // peers, i % peers

        @pl.when(j != me)
        def _():
            spectra_copy(c, region, j, j, j).wait_send()
            grad_copy(c, region, j, j, j).wait_send()

        @pl.when(region > 0)
        def _():
            spectra_copy(c, region, peers + j, peers + j, j).wait_send()

        @pl.when(region < last)
        def _():
            grad_copy(c, region, peers + j, peers + j, j).wait_send()

        return carry

    lax.fori_loop(0, 3 * peers, sent, 0)

    @pl.when(region < last)
    def _():
        idx_copy(region).wait_send()


def on_device(
    regions, peers, synthetic, observed, nearby, far_rows, first, second, start, length
):
    local, _, ticks = synthetic.shape
    cap = nearby.shape[1]
    pairs = first.shape[0]
    forward, lag = make_tables(ticks)
    middle, width = ticks // 2, 512
    forward = forward[:middle].reshape(middle, 2, F // 2, 2).transpose(3, 1, 2, 0)
    lag = lag.reshape(2, F // 2, 2, LAGS).transpose(0, 2, 1, 3).reshape(2 * F, LAGS)
    plain = lambda a: jnp.asarray(np.ascontiguousarray(a))
    w = plain(forward.reshape(4, BLOCK, middle).transpose(0, 2, 1))
    wt = plain(forward.reshape(2, F, middle // width, width).transpose(2, 0, 1, 3))
    lagt = plain(lag.T)
    lag = plain(lag)
    sources = 2 * peers
    rows = sources * 16
    vmem = pl.BlockSpec(memory_space=pltpu.VMEM)
    hbm = pl.BlockSpec(memory_space=pl.ANY)
    b16, f32 = jnp.bfloat16, jnp.float32
    adj, misfit = pl.pallas_call(
        functools.partial(kernel, regions, peers, cap, local),
        out_shape=(
            jax.ShapeDtypeStruct((3 * local, ticks), b16),
            jax.ShapeDtypeStruct((1, pairs), f32),
        ),
        in_specs=[vmem] * 8 + [hbm] * 4,
        out_specs=(vmem, vmem),
        scratch_shapes=[
            pltpu.VMEM(w.shape, b16),
            pltpu.VMEM(wt.shape, b16),
            pltpu.VMEM(lag.shape, b16),
            pltpu.VMEM(lagt.shape, b16),
            pltpu.VMEM((cap, peers), jnp.int32),
            pltpu.VMEM((3, 4 * local, F), b16),
            pltpu.VMEM((3, sources, 16, F), b16),
            pltpu.VMEM((3, sources, 16, F), b16),
            pltpu.VMEM((3, sources, 16, BLOCK), b16),
            pltpu.VMEM((3, sources, 16, BLOCK), b16),
            pltpu.VMEM((2, 3, local, F), b16),
            pltpu.VMEM((8 * pairs, rows), b16),
            pltpu.VMEM((rows, 8 * pairs), b16),
            pltpu.VMEM((rows, 64), b16),
            pltpu.VMEM((64, rows), b16),
            pltpu.VMEM((pairs, LAGS), f32),
            pltpu.VMEM((pairs, LAGS), f32),
            pltpu.VMEM((8 * pairs, BLOCK), b16),
            pltpu.VMEM((8, pairs, F), b16),
            pltpu.VMEM((pairs, 2 * F), b16),
            pltpu.VMEM((pairs, 2 * F), f32),
            pltpu.SemaphoreType.DMA((4,)),
            pltpu.SemaphoreType.DMA((3,)),
            pltpu.SemaphoreType.DMA,
            pltpu.SemaphoreType.DMA,
            pltpu.SemaphoreType.DMA((3, sources)),
            pltpu.SemaphoreType.DMA((3, sources)),
            pltpu.SemaphoreType.DMA((3, sources)),
            pltpu.SemaphoreType.DMA((3, sources)),
        ],
        compiler_params=pltpu.CompilerParams(
            collective_id=0, has_side_effects=True, vmem_limit_bytes=60 * 1024 * 1024
        ),
    )(
        synthetic.transpose(1, 0, 2), observed.transpose(1, 0, 2), nearby.T, far_rows.T,
        first.reshape(1, pairs), second.reshape(1, pairs),
        start.reshape(1, pairs), length.reshape(1, pairs), w, wt, lag, lagt,
    )
    return adj.reshape(3, local, ticks).transpose(1, 0, 2), misfit.reshape(pairs)


def solution(mesh):
    placed = (P(("region", "dev"), None, None),) * 2 + (P(("region", "dev"), None),) * 2
    placed += (P(("region", "dev")),) * 4
    return jax.shard_map(
        functools.partial(on_device, mesh.shape["region"], mesh.shape["dev"]),
        mesh=mesh,
        in_specs=placed,
        out_specs=(P(("region", "dev"), None, None), P(("region", "dev"))),
        check_vma=False,
    )
```

```python
import functools
import math

import jax
import jax.numpy as jnp
import ml_dtypes
import numpy as np
from jax import lax
from jax.experimental import pallas as pl
from jax.experimental.pallas import tpu as pltpu
from jax.sharding import PartitionSpec as P

F = 512
FLOW = 64
LAGS = 512
BLOCK = 256
MESH = pl.DeviceIdType.MESH


def make_tables(ticks):
    rate = FLOW + np.arange(F, dtype=np.int64)
    angles = (np.arange(ticks)[:, None] * rate[None, :] % ticks) * (2.0 * math.pi / ticks)
    forward = np.concatenate([np.cos(angles), -np.sin(angles)], 1) / math.sqrt(ticks)
    shifts = np.arange(LAGS, dtype=np.int64) - LAGS // 2
    turning = (rate[:, None] * shifts[None, :] % ticks) * (2.0 * math.pi / ticks)
    lag = np.concatenate([np.cos(turning), -np.sin(turning)], 0) / math.sqrt(F)
    short = lambda x: x.astype(np.float32).astype(ml_dtypes.bfloat16)
    return short(forward), short(lag)


def dot(a, b):
    return jnp.dot(a, b, preferred_element_type=jnp.float32)


def one_hot(condition):
    return jnp.where(condition, 1.0, 0.0).astype(jnp.bfloat16)


def iota(shape, axis):
    return lax.broadcasted_iota(jnp.int32, shape, axis)


def down(row, width):
    pairs = row.shape[1]
    column = jnp.transpose(jnp.broadcast_to(row.astype(jnp.float32), (128, pairs)))
    return jnp.concatenate([column] * (width // 128), 1).astype(jnp.int32)


def kernel(
    regions, peers, cap, local,
    syn_ref, obs_ref, near_ref, far_ref, first_ref, second_ref, start_ref, length_ref,
    w_hbm, wt_hbm, lag_hbm, lagt_hbm,
    adj_ref, misfit_ref,
    w, wt, lag, lagt, far_in, sp, send, recv, gout, gin, own, pick, spread, sel_out, sel_in,
    inside, energy, grads,
    w_sem, table_sem, idx_send, idx_recv, send_sem, recv_sem, gsend_sem, grecv_sem,
):
    region, me = lax.axis_index("region"), lax.axis_index("dev")
    last = regions - 1
    sources = 2 * peers
    rows = sources * 16
    pairs = first_ref.shape[1]

    w_copies = [pltpu.make_async_copy(w_hbm.at[i], w.at[i], w_sem.at[i]) for i in range(4)]
    table_copies = [
        pltpu.make_async_copy(a, b, table_sem.at[i])
        for i, (a, b) in enumerate(((lag_hbm, lag), (lagt_hbm, lagt), (wt_hbm, wt)))
    ]
    for copy in w_copies + table_copies:
        copy.start()

    barrier = pltpu.get_barrier_semaphore()

    def greet(j, carry):
        @pl.when(j != me)
        def _():
            pl.semaphore_signal(barrier, inc=1, device_id=(region, j), device_id_type=MESH)

        @pl.when(region > 0)
        def _():
            pl.semaphore_signal(barrier, inc=1, device_id=(region - 1, j), device_id_type=MESH)

        @pl.when(region < last)
        def _():
            pl.semaphore_signal(barrier, inc=1, device_id=(region + 1, j), device_id_type=MESH)

        return carry

    lax.fori_loop(0, peers, greet, 0)
    below = jnp.where(region > 0, peers, 0)
    above = jnp.where(region < last, peers, 0)
    pl.semaphore_wait(barrier, peers - 1 + below + above)

    def idx_copy(target):
        return pltpu.make_async_remote_copy(
            src_ref=far_ref, dst_ref=far_in, send_sem=idx_send, recv_sem=idx_recv,
            device_id=(target, me), device_id_type=MESH,
        )

    @pl.when(region < last)
    def _():
        idx_copy(region + 1).start()

    @pl.when(region == 0)
    def _():
        far_in[...] = jnp.zeros_like(far_in)
        gin[:, peers:sources] = jnp.zeros((3, peers, 16, BLOCK), jnp.bfloat16)

    @pl.when(region == last)
    def _():
        recv[:, peers:sources] = jnp.zeros((3, peers, 16, F), jnp.bfloat16)

    count = 6 * local
    x = jnp.concatenate(
        [syn_ref[...].reshape(3 * local, -1), obs_ref[...].reshape(3 * local, -1)], 0
    ).astype(jnp.float32)
    middle = x.shape[1] // 2
    def transform(half):
        x0, x1 = x[:, :middle], x[:, middle:]
        folded = x0 - x1 if half else x0 + x1
        high = folded.astype(jnp.bfloat16)
        low = (folded - high.astype(jnp.float32)).astype(jnp.bfloat16)
        both = jnp.concatenate([high, low], 0)
        for part in range(2):
            w_copies[half * 2 + part].wait()
            y = dot(both, w[half * 2 + part])
            y = (y[:count] + y[count:]).astype(jnp.bfloat16)
            for k in range(2):
                for c in range(3):
                    at = part * 32 + k * 16
                    sp[c, at : at + 16, half * BLOCK : (half + 1) * BLOCK] = y[
                        k * 48 + c * 16 : k * 48 + c * 16 + 16
                    ]

    transform(0)

    @pl.when(region > 0)
    def _():
        idx_copy(region).wait_recv()

    near_owner = jnp.where(iota((peers, rows), 1) // 16 == iota((peers, rows), 0), 1.0, 0.0)
    far_owner = jnp.where(
        iota((peers, rows), 1) // 16 == iota((peers, rows), 0) + peers, 1.0, 0.0
    )
    wide = dot(near_ref[...].astype(jnp.float32), near_owner)
    wide += dot(far_in[...].astype(jnp.float32), far_owner)
    wide = jnp.where(iota((cap, rows), 1) % 4 == iota((cap, rows), 0), wide, 0.0)
    asked_row = jnp.broadcast_to(jnp.sum(wide, 0, keepdims=True), (128, rows))
    asked_col = jnp.transpose(asked_row)
    asked_row = asked_row[:64].astype(jnp.int32)
    row = iota((rows, 64), 0)
    column = (row // 4 % 2) * 32 + (row // 8 % 2) * 16 + asked_col[:, :64].astype(jnp.int32)
    sel_out[...] = one_hot(column == iota((rows, 64), 1))
    up = iota((64, rows), 0)
    sel_in[...] = one_hot((asked_row == up % 16) & (iota((64, rows), 1) // 4 % 4 == up // 16))

    def spectra_copy(group, to, src, dst, target):
        if isinstance(group, int) and group < 2:
            columns = pl.ds(group * BLOCK, BLOCK)
            source, landing = send.at[0, src, :, columns], recv.at[0, dst, :, columns]
        else:
            source, landing = send.at[group - 1, src], recv.at[group - 1, dst]
        return pltpu.make_async_remote_copy(
            src_ref=source, dst_ref=landing,
            send_sem=send_sem.at[group, src], recv_sem=recv_sem.at[group, dst],
            device_id=(to, target), device_id_type=MESH,
        )

    def grad_copy(c, to, src, dst, target):
        return pltpu.make_async_remote_copy(
            src_ref=gout.at[c, src], dst_ref=gin.at[c, dst],
            send_sem=gsend_sem.at[c, src], recv_sem=grecv_sem.at[c, dst],
            device_id=(to, target), device_id_type=MESH,
        )

    def exchange(group):
        c = max(group - 1, 0)
        columns = pl.ds(group * BLOCK, BLOCK) if group < 2 else pl.ds(0, F)
        block = dot(sel_out[...], sp[c, :, columns]).astype(jnp.bfloat16)
        send[c, :, :, columns] = block.reshape(sources, 16, -1)
        recv[c, me, :, columns] = send[c, me, :, columns]

        def go(i, carry):
            j = (me + 1 + i) % peers

            @pl.when(j != me)
            def _():
                spectra_copy(group, region, j, me, j).start()

            @pl.when(region > 0)
            def _():
                spectra_copy(group, region - 1, peers + j, peers + me, j).start()

            return carry

        lax.fori_loop(0, peers, go, 0)

    exchange(0)
    transform(1)
    for group in range(1, 4):
        exchange(group)

    for end, ref in enumerate((first_ref, second_ref)):
        slot = ref[...]
        base = (slot >> 2) * 16 + (slot & 3)
        column = down(base, rows)
        lanes = iota((pairs, rows), 1)
        ups = iota((rows, pairs), 0)
        for o in range(4):
            at = (end * 4 + o) * pairs
            pick[at : at + pairs, :] = one_hot(lanes == column + 4 * o)
            spread[:, at : at + pairs] = one_hot(ups == base + 4 * o)
    position = iota((pairs, LAGS), 1)
    begin = down(start_ref[...], LAGS)
    stop = down(start_ref[...] + length_ref[...], LAGS)
    inside[...] = jnp.where((position >= begin) & (position < stop), 1.0, 0.0)
    energy[...] = jnp.zeros_like(energy)

    table_copies[0].wait()
    table_copies[1].wait()

    def work(c, carry):
        def arrive(j, carry):
            def take(group):
                @pl.when(j != me)
                def _():
                    spectra_copy(group, region, j, j, j).wait_recv()

                @pl.when(region < last)
                def _():
                    spectra_copy(group, region, peers + j, peers + j, j).wait_recv()

            @pl.when(c == 0)
            def _():
                take(0)
                take(1)

            @pl.when(c > 0)
            def _():
                take(c + 1)

            return carry

        lax.fori_loop(0, peers, arrive, 0)
        fetched = recv[c].reshape(rows, F)
        got = lambda end, o: dot(pick[(end * 4 + o) * pairs : (end * 4 + o + 1) * pairs], fetched)
        ar, ai, br, bi = got(0, 0), got(0, 1), got(1, 0), got(1, 1)
        ur, ui, vr, vi = got(0, 2), got(0, 3), got(1, 2), got(1, 3)
        change_re = ((ar * br + ai * bi) - (ur * vr + ui * vi)).astype(jnp.bfloat16)
        change_im = ((ai * br - ar * bi) - (ui * vr - ur * vi)).astype(jnp.bfloat16)
        shifted = dot(change_re, lag[:F]) + dot(change_im, lag[F:])
        residual = jnp.where(inside[...] > 0.5, shifted, 0.0)
        energy[...] += residual * residual
        short = residual.astype(jnp.bfloat16)
        gr, gi = dot(short, lagt[:, :F]), dot(short, lagt[:, F:])
        ends = (
            (gr * br - gi * bi, gr * bi + gi * br),
            (gr * ar + gi * ai, gr * ai - gi * ar),
        )
        for end in range(2):
            for part in range(2):
                value = ends[end][part].astype(jnp.bfloat16)
                for half in range(2):
                    at = (end * 4 + half * 2 + part) * pairs
                    grads[at : at + pairs] = value[:, half * BLOCK : (half + 1) * BLOCK]
        total = dot(spread[...], grads[...]).astype(jnp.bfloat16)
        gout[c] = total.reshape(sources, 16, BLOCK)
        gin[c, me] = gout[c, me]

        def go(i, carry):
            j = (me + 1 + i) % peers

            @pl.when(j != me)
            def _():
                grad_copy(c, region, j, me, j).start()

            @pl.when(region < last)
            def _():
                grad_copy(c, region + 1, peers + j, peers + me, j).start()

            return carry

        return lax.fori_loop(0, peers, go, carry)

    lax.fori_loop(0, 3, work, 0)

    power = energy[:, :128]
    for i in range(1, LAGS // 128):
        power = power + energy[:, i * 128 : (i + 1) * 128]
    misfit_ref[...] = jnp.sum(jnp.transpose(power), 0, keepdims=True) / (2.0 * LAGS)

    def settle(c, carry):
        def arrive(j, carry):
            @pl.when(j != me)
            def _():
                grad_copy(c, region, j, j, j).wait_recv()

            @pl.when(region > 0)
            def _():
                grad_copy(c, region, peers + j, peers + j, j).wait_recv()

            return carry

        lax.fori_loop(0, peers, arrive, 0)
        total = dot(sel_in[...], gin[c].reshape(rows, BLOCK)).astype(jnp.bfloat16)
        for half in range(2):
            for part in range(2):
                o = half * 2 + part
                own[half, c, :, part * BLOCK : (part + 1) * BLOCK] = total[o * 16 : o * 16 + 16]
        return carry

    lax.fori_loop(0, 3, settle, 0)

    table_copies[2].wait()
    even = own[0].reshape(3 * local, F)
    odd = own[1].reshape(3 * local, F)
    width = wt.shape[3]

    def back(i, carry):
        at = pl.multiple_of(i * width, width)
        plain, signed = dot(even, wt[i, 0]), dot(odd, wt[i, 1])
        adj_ref[:, pl.ds(at, width)] = (plain + signed).astype(jnp.bfloat16)
        adj_ref[:, pl.ds(at + middle, width)] = (plain - signed).astype(jnp.bfloat16)
        return carry

    lax.fori_loop(0, wt.shape[0], back, 0)

    def sent(j, carry):
        for c in range(3):
            @pl.when(j != me)
            def _():
                grad_copy(c, region, j, j, j).wait_send()

            @pl.when(region < last)
            def _():
                grad_copy(c, region, peers + j, peers + j, j).wait_send()

        for group in range(4):
            @pl.when(j != me)
            def _():
                spectra_copy(group, region, j, j, j).wait_send()

            @pl.when(region > 0)
            def _():
                spectra_copy(group, region, peers + j, peers + j, j).wait_send()

        return carry

    lax.fori_loop(0, peers, sent, 0)

    @pl.when(region < last)
    def _():
        idx_copy(region).wait_send()


def on_device(
    regions, peers, synthetic, observed, nearby, far_rows, first, second, start, length
):
    local, _, ticks = synthetic.shape
    cap = nearby.shape[1]
    pairs = first.shape[0]
    forward, lag = make_tables(ticks)
    middle, width = ticks // 2, 512
    forward = forward[:middle].reshape(middle, 2, F // 2, 2).transpose(3, 1, 2, 0)
    lag = lag.reshape(2, F // 2, 2, LAGS).transpose(0, 2, 1, 3).reshape(2 * F, LAGS)
    plain = lambda a: jnp.asarray(np.ascontiguousarray(a))
    w = plain(forward.reshape(4, BLOCK, middle).transpose(0, 2, 1))
    wt = plain(forward.reshape(2, F, middle // width, width).transpose(2, 0, 1, 3))
    lagt = plain(lag.T)
    lag = plain(lag)
    sources = 2 * peers
    rows = sources * 16
    vmem = pl.BlockSpec(memory_space=pltpu.VMEM)
    hbm = pl.BlockSpec(memory_space=pl.ANY)
    b16, f32 = jnp.bfloat16, jnp.float32
    adj, misfit = pl.pallas_call(
        functools.partial(kernel, regions, peers, cap, local),
        out_shape=(
            jax.ShapeDtypeStruct((3 * local, ticks), b16),
            jax.ShapeDtypeStruct((1, pairs), f32),
        ),
        in_specs=[vmem] * 8 + [hbm] * 4,
        out_specs=(vmem, vmem),
        scratch_shapes=[
            pltpu.VMEM(w.shape, b16),
            pltpu.VMEM(wt.shape, b16),
            pltpu.VMEM(lag.shape, b16),
            pltpu.VMEM(lagt.shape, b16),
            pltpu.VMEM((cap, peers), jnp.int32),
            pltpu.VMEM((3, 4 * local, F), b16),
            pltpu.VMEM((3, sources, 16, F), b16),
            pltpu.VMEM((3, sources, 16, F), b16),
            pltpu.VMEM((3, sources, 16, BLOCK), b16),
            pltpu.VMEM((3, sources, 16, BLOCK), b16),
            pltpu.VMEM((2, 3, local, F), b16),
            pltpu.VMEM((8 * pairs, rows), b16),
            pltpu.VMEM((rows, 8 * pairs), b16),
            pltpu.VMEM((rows, 64), b16),
            pltpu.VMEM((64, rows), b16),
            pltpu.VMEM((pairs, LAGS), f32),
            pltpu.VMEM((pairs, LAGS), f32),
            pltpu.VMEM((8 * pairs, BLOCK), b16),
            pltpu.SemaphoreType.DMA((4,)),
            pltpu.SemaphoreType.DMA((3,)),
            pltpu.SemaphoreType.DMA,
            pltpu.SemaphoreType.DMA,
            pltpu.SemaphoreType.DMA((4, sources)),
            pltpu.SemaphoreType.DMA((4, sources)),
            pltpu.SemaphoreType.DMA((3, sources)),
            pltpu.SemaphoreType.DMA((3, sources)),
        ],
        compiler_params=pltpu.CompilerParams(
            collective_id=0, has_side_effects=True, vmem_limit_bytes=60 * 1024 * 1024
        ),
    )(
        synthetic.transpose(1, 0, 2), observed.transpose(1, 0, 2), nearby.T, far_rows.T,
        first.reshape(1, pairs), second.reshape(1, pairs),
        start.reshape(1, pairs), length.reshape(1, pairs), w, wt, lag, lagt,
    )
    return adj.reshape(3, local, ticks).transpose(1, 0, 2), misfit.reshape(pairs)


def solution(mesh):
    placed = (P(("region", "dev"), None, None),) * 2 + (P(("region", "dev"), None),) * 2
    placed += (P(("region", "dev")),) * 4
    return jax.shard_map(
        functools.partial(on_device, mesh.shape["region"], mesh.shape["dev"]),
        mesh=mesh,
        in_specs=placed,
        out_specs=(P(("region", "dev"), None, None), P(("region", "dev"))),
        check_vma=False,
    )
```

```python
import functools
import math

import jax
import jax.numpy as jnp
import ml_dtypes
import numpy as np
from jax import lax
from jax.experimental import pallas as pl
from jax.experimental.pallas import tpu as pltpu
from jax.sharding import PartitionSpec as P

F = 512
FLOW = 64
LAGS = 512
BLOCK = 256
MESH = pl.DeviceIdType.MESH


def make_tables(ticks):
    rate = FLOW + np.arange(F, dtype=np.int64)
    angles = (np.arange(ticks)[:, None] * rate[None, :] % ticks) * (2.0 * math.pi / ticks)
    forward = np.concatenate([np.cos(angles), -np.sin(angles)], 1) / math.sqrt(ticks)
    shifts = np.arange(LAGS, dtype=np.int64) - LAGS // 2
    turning = (rate[:, None] * shifts[None, :] % ticks) * (2.0 * math.pi / ticks)
    lag = np.concatenate([np.cos(turning), -np.sin(turning)], 0) / math.sqrt(F)
    short = lambda x: x.astype(np.float32).astype(ml_dtypes.bfloat16)
    return short(forward), short(lag)


def dot(a, b):
    return jnp.dot(a, b, preferred_element_type=jnp.float32)


def one_hot(condition):
    return jnp.where(condition, 1.0, 0.0).astype(jnp.bfloat16)


def iota(shape, axis):
    return lax.broadcasted_iota(jnp.int32, shape, axis)


def down(row, width):
    pairs = row.shape[1]
    column = jnp.transpose(jnp.broadcast_to(row.astype(jnp.float32), (128, pairs)))
    return jnp.concatenate([column] * (width // 128), 1).astype(jnp.int32)


def kernel(
    regions, peers, cap, local,
    syn_ref, obs_ref, near_ref, far_ref, first_ref, second_ref, start_ref, length_ref,
    w_hbm, wt_hbm, lag_hbm, lagt_hbm,
    adj_ref, misfit_ref,
    w, wt, lag, lagt, far_in, sp, send, recv, gout, gin, own, pick, spread, sel_out, sel_in,
    inside, energy, grads,
    w_sem, table_sem, idx_send, idx_recv, send_sem, recv_sem, gsend_sem, grecv_sem,
):
    region, me = lax.axis_index("region"), lax.axis_index("dev")
    last = regions - 1
    sources = 2 * peers
    rows = sources * 16
    pairs = first_ref.shape[1]

    w_copies = [pltpu.make_async_copy(w_hbm.at[i], w.at[i], w_sem.at[i]) for i in range(4)]
    table_copies = [
        pltpu.make_async_copy(a, b, table_sem.at[i])
        for i, (a, b) in enumerate(((lag_hbm, lag), (lagt_hbm, lagt), (wt_hbm, wt)))
    ]
    for copy in w_copies + table_copies:
        copy.start()

    barrier = pltpu.get_barrier_semaphore()

    def greet(j, carry):
        @pl.when(j != me)
        def _():
            pl.semaphore_signal(barrier, inc=1, device_id=(region, j), device_id_type=MESH)

        @pl.when(region > 0)
        def _():
            pl.semaphore_signal(barrier, inc=1, device_id=(region - 1, j), device_id_type=MESH)

        @pl.when(region < last)
        def _():
            pl.semaphore_signal(barrier, inc=1, device_id=(region + 1, j), device_id_type=MESH)

        return carry

    lax.fori_loop(0, peers, greet, 0)
    below = jnp.where(region > 0, peers, 0)
    above = jnp.where(region < last, peers, 0)
    pl.semaphore_wait(barrier, peers - 1 + below + above)

    def idx_copy(target):
        return pltpu.make_async_remote_copy(
            src_ref=far_ref, dst_ref=far_in, send_sem=idx_send, recv_sem=idx_recv,
            device_id=(target, me), device_id_type=MESH,
        )

    @pl.when(region < last)
    def _():
        idx_copy(region + 1).start()

    @pl.when(region == 0)
    def _():
        far_in[...] = jnp.zeros_like(far_in)
        gin[:, peers:sources] = jnp.zeros((3, peers, 16, BLOCK), jnp.bfloat16)

    @pl.when(region == last)
    def _():
        recv[:, peers:sources] = jnp.zeros((3, peers, 16, F), jnp.bfloat16)

    count = 6 * local
    x = jnp.concatenate(
        [syn_ref[...].reshape(3 * local, -1), obs_ref[...].reshape(3 * local, -1)], 0
    ).astype(jnp.float32)
    middle = x.shape[1] // 2
    for half in range(2):
        x0, x1 = x[:, :middle], x[:, middle:]
        folded = x0 - x1 if half else x0 + x1
        high = folded.astype(jnp.bfloat16)
        low = (folded - high.astype(jnp.float32)).astype(jnp.bfloat16)
        both = jnp.concatenate([high, low], 0)
        for part in range(2):
            w_copies[half * 2 + part].wait()
            y = dot(both, w[half * 2 + part])
            y = (y[:count] + y[count:]).astype(jnp.bfloat16)
            for k in range(2):
                for c in range(3):
                    at = part * 32 + k * 16
                    sp[c, at : at + 16, half * BLOCK : (half + 1) * BLOCK] = y[
                        k * 48 + c * 16 : k * 48 + c * 16 + 16
                    ]

    @pl.when(region > 0)
    def _():
        idx_copy(region).wait_recv()

    near_owner = jnp.where(iota((peers, rows), 1) // 16 == iota((peers, rows), 0), 1.0, 0.0)
    far_owner = jnp.where(
        iota((peers, rows), 1) // 16 == iota((peers, rows), 0) + peers, 1.0, 0.0
    )
    wide = dot(near_ref[...].astype(jnp.float32), near_owner)
    wide += dot(far_in[...].astype(jnp.float32), far_owner)
    wide = jnp.where(iota((cap, rows), 1) % 4 == iota((cap, rows), 0), wide, 0.0)
    asked_row = jnp.broadcast_to(jnp.sum(wide, 0, keepdims=True), (128, rows))
    asked_col = jnp.transpose(asked_row)
    asked_row = asked_row[:64].astype(jnp.int32)
    row = iota((rows, 64), 0)
    column = (row // 4 % 2) * 32 + (row // 8 % 2) * 16 + asked_col[:, :64].astype(jnp.int32)
    sel_out[...] = one_hot(column == iota((rows, 64), 1))
    up = iota((64, rows), 0)
    sel_in[...] = one_hot((asked_row == up % 16) & (iota((64, rows), 1) // 4 % 4 == up // 16))

    def spectra_copy(c, to, src, dst, target):
        return pltpu.make_async_remote_copy(
            src_ref=send.at[c, src], dst_ref=recv.at[c, dst],
            send_sem=send_sem.at[c, src], recv_sem=recv_sem.at[c, dst],
            device_id=(to, target), device_id_type=MESH,
        )

    def grad_copy(c, to, src, dst, target):
        return pltpu.make_async_remote_copy(
            src_ref=gout.at[c, src], dst_ref=gin.at[c, dst],
            send_sem=gsend_sem.at[c, src], recv_sem=grecv_sem.at[c, dst],
            device_id=(to, target), device_id_type=MESH,
        )

    def exchange(c, carry):
        block = dot(sel_out[...], sp[c]).astype(jnp.bfloat16)
        send[c] = block.reshape(sources, 16, F)
        recv[c, me] = send[c, me]

        def go(i, carry):
            j = (me + peers // 2 + i) % peers

            @pl.when(j != me)
            def _():
                spectra_copy(c, region, j, me, j).start()

            @pl.when(region > 0)
            def _():
                spectra_copy(c, region - 1, peers + j, peers + me, j).start()

            return carry

        return lax.fori_loop(0, peers, go, carry)

    lax.fori_loop(0, 3, exchange, 0)

    for end, ref in enumerate((first_ref, second_ref)):
        slot = ref[...]
        base = (slot >> 2) * 16 + (slot & 3)
        column = down(base, rows)
        lanes = iota((pairs, rows), 1)
        ups = iota((rows, pairs), 0)
        for o in range(4):
            at = (end * 4 + o) * pairs
            pick[at : at + pairs, :] = one_hot(lanes == column + 4 * o)
            spread[:, at : at + pairs] = one_hot(ups == base + 4 * o)
    position = iota((pairs, LAGS), 1)
    begin = down(start_ref[...], LAGS)
    stop = down(start_ref[...] + length_ref[...], LAGS)
    inside[...] = jnp.where((position >= begin) & (position < stop), 1.0, 0.0)
    energy[...] = jnp.zeros_like(energy)

    table_copies[0].wait()
    table_copies[1].wait()

    def work(c, carry):
        def arrive(j, carry):
            @pl.when(j != me)
            def _():
                spectra_copy(c, region, j, j, j).wait_recv()

            @pl.when(region < last)
            def _():
                spectra_copy(c, region, peers + j, peers + j, j).wait_recv()

            return carry

        lax.fori_loop(0, peers, arrive, 0)
        fetched = recv[c].reshape(rows, F)
        got = lambda end, o: dot(pick[(end * 4 + o) * pairs : (end * 4 + o + 1) * pairs], fetched)
        ar, ai, br, bi = got(0, 0), got(0, 1), got(1, 0), got(1, 1)
        ur, ui, vr, vi = got(0, 2), got(0, 3), got(1, 2), got(1, 3)
        change_re = ((ar * br + ai * bi) - (ur * vr + ui * vi)).astype(jnp.bfloat16)
        change_im = ((ai * br - ar * bi) - (ui * vr - ur * vi)).astype(jnp.bfloat16)
        shifted = dot(change_re, lag[:F]) + dot(change_im, lag[F:])
        residual = jnp.where(inside[...] > 0.5, shifted, 0.0)
        energy[...] += residual * residual
        short = residual.astype(jnp.bfloat16)
        gr, gi = dot(short, lagt[:, :F]), dot(short, lagt[:, F:])
        ends = (
            (gr * br - gi * bi, gr * bi + gi * br),
            (gr * ar + gi * ai, gr * ai - gi * ar),
        )
        for end in range(2):
            for part in range(2):
                value = ends[end][part].astype(jnp.bfloat16)
                for half in range(2):
                    at = (end * 4 + half * 2 + part) * pairs
                    grads[at : at + pairs] = value[:, half * BLOCK : (half + 1) * BLOCK]
        total = dot(spread[...], grads[...]).astype(jnp.bfloat16)
        gout[c] = total.reshape(sources, 16, BLOCK)
        gin[c, me] = gout[c, me]

        def go(i, carry):
            j = (me + peers // 2 + i) % peers

            @pl.when(j != me)
            def _():
                grad_copy(c, region, j, me, j).start()

            @pl.when(region < last)
            def _():
                grad_copy(c, region + 1, peers + j, peers + me, j).start()

            return carry

        return lax.fori_loop(0, peers, go, carry)

    lax.fori_loop(0, 3, work, 0)

    power = energy[:, :128]
    for i in range(1, LAGS // 128):
        power = power + energy[:, i * 128 : (i + 1) * 128]
    misfit_ref[...] = jnp.sum(jnp.transpose(power), 0, keepdims=True) / (2.0 * LAGS)

    def settle(c, carry):
        def arrive(j, carry):
            @pl.when(j != me)
            def _():
                grad_copy(c, region, j, j, j).wait_recv()

            @pl.when(region > 0)
            def _():
                grad_copy(c, region, peers + j, peers + j, j).wait_recv()

            return carry

        lax.fori_loop(0, peers, arrive, 0)
        total = dot(sel_in[...], gin[c].reshape(rows, BLOCK)).astype(jnp.bfloat16)
        for half in range(2):
            for part in range(2):
                o = half * 2 + part
                own[half, c, :, part * BLOCK : (part + 1) * BLOCK] = total[o * 16 : o * 16 + 16]
        return carry

    lax.fori_loop(0, 3, settle, 0)

    table_copies[2].wait()
    even = own[0].reshape(3 * local, F)
    odd = own[1].reshape(3 * local, F)
    width = wt.shape[3]

    def back(i, carry):
        at = pl.multiple_of(i * width, width)
        plain, signed = dot(even, wt[i, 0]), dot(odd, wt[i, 1])
        adj_ref[:, pl.ds(at, width)] = (plain + signed).astype(jnp.bfloat16)
        adj_ref[:, pl.ds(at + middle, width)] = (plain - signed).astype(jnp.bfloat16)
        return carry

    lax.fori_loop(0, wt.shape[0], back, 0)

    def sent(i, carry):
        c, j = i // peers, i % peers

        @pl.when(j != me)
        def _():
            spectra_copy(c, region, j, j, j).wait_send()
            grad_copy(c, region, j, j, j).wait_send()

        @pl.when(region > 0)
        def _():
            spectra_copy(c, region, peers + j, peers + j, j).wait_send()

        @pl.when(region < last)
        def _():
            grad_copy(c, region, peers + j, peers + j, j).wait_send()

        return carry

    lax.fori_loop(0, 3 * peers, sent, 0)

    @pl.when(region < last)
    def _():
        idx_copy(region).wait_send()


def on_device(
    regions, peers, synthetic, observed, nearby, far_rows, first, second, start, length
):
    local, _, ticks = synthetic.shape
    cap = nearby.shape[1]
    pairs = first.shape[0]
    forward, lag = make_tables(ticks)
    middle, width = ticks // 2, 512
    forward = forward[:middle].reshape(middle, 2, F // 2, 2).transpose(3, 1, 2, 0)
    lag = lag.reshape(2, F // 2, 2, LAGS).transpose(0, 2, 1, 3).reshape(2 * F, LAGS)
    plain = lambda a: jnp.asarray(np.ascontiguousarray(a))
    w = plain(forward.reshape(4, BLOCK, middle).transpose(0, 2, 1))
    wt = plain(forward.reshape(2, F, middle // width, width).transpose(2, 0, 1, 3))
    lagt = plain(lag.T)
    lag = plain(lag)
    sources = 2 * peers
    rows = sources * 16
    vmem = pl.BlockSpec(memory_space=pltpu.VMEM)
    hbm = pl.BlockSpec(memory_space=pl.ANY)
    b16, f32 = jnp.bfloat16, jnp.float32
    adj, misfit = pl.pallas_call(
        functools.partial(kernel, regions, peers, cap, local),
        out_shape=(
            jax.ShapeDtypeStruct((3 * local, ticks), b16),
            jax.ShapeDtypeStruct((1, pairs), f32),
        ),
        in_specs=[vmem] * 8 + [hbm] * 4,
        out_specs=(vmem, vmem),
        scratch_shapes=[
            pltpu.VMEM(w.shape, b16),
            pltpu.VMEM(wt.shape, b16),
            pltpu.VMEM(lag.shape, b16),
            pltpu.VMEM(lagt.shape, b16),
            pltpu.VMEM((cap, peers), jnp.int32),
            pltpu.VMEM((3, 4 * local, F), b16),
            pltpu.VMEM((3, sources, 16, F), b16),
            pltpu.VMEM((3, sources, 16, F), b16),
            pltpu.VMEM((3, sources, 16, BLOCK), b16),
            pltpu.VMEM((3, sources, 16, BLOCK), b16),
            pltpu.VMEM((2, 3, local, F), b16),
            pltpu.VMEM((8 * pairs, rows), b16),
            pltpu.VMEM((rows, 8 * pairs), b16),
            pltpu.VMEM((rows, 64), b16),
            pltpu.VMEM((64, rows), b16),
            pltpu.VMEM((pairs, LAGS), f32),
            pltpu.VMEM((pairs, LAGS), f32),
            pltpu.VMEM((8 * pairs, BLOCK), b16),
            pltpu.SemaphoreType.DMA((4,)),
            pltpu.SemaphoreType.DMA((3,)),
            pltpu.SemaphoreType.DMA,
            pltpu.SemaphoreType.DMA,
            pltpu.SemaphoreType.DMA((3, sources)),
            pltpu.SemaphoreType.DMA((3, sources)),
            pltpu.SemaphoreType.DMA((3, sources)),
            pltpu.SemaphoreType.DMA((3, sources)),
        ],
        compiler_params=pltpu.CompilerParams(
            collective_id=0, has_side_effects=True, vmem_limit_bytes=60 * 1024 * 1024
        ),
    )(
        synthetic.transpose(1, 0, 2), observed.transpose(1, 0, 2), nearby.T, far_rows.T,
        first.reshape(1, pairs), second.reshape(1, pairs),
        start.reshape(1, pairs), length.reshape(1, pairs), w, wt, lag, lagt,
    )
    return adj.reshape(3, local, ticks).transpose(1, 0, 2), misfit.reshape(pairs)


def solution(mesh):
    placed = (P(("region", "dev"), None, None),) * 2 + (P(("region", "dev"), None),) * 2
    placed += (P(("region", "dev")),) * 4
    return jax.shard_map(
        functools.partial(on_device, mesh.shape["region"], mesh.shape["dev"]),
        mesh=mesh,
        in_specs=placed,
        out_specs=(P(("region", "dev"), None, None), P(("region", "dev"))),
        check_vma=False,
    )
```
